256 devices in a mesh: seq: 64 (over z, x, core), head: 4 (over y).
Axes of the slice: x: 4, y: 4, z: 8, core: 2. Of those that a mesh axis runs over, the one named last changes fastest.
Arguments:
- x_in: bfloat16 [24576, 8192], P('seq', 'head'), may hold values from -6 to 6
- bc_in: bfloat16 [24576, 2, 1024], P('seq', None, 'head'), may hold values from -6 to 6
- gate_in: bfloat16 [24576, 8192], P('seq', 'head'), may hold values from -6 to 6
- step_size: float32 [24576, 128], P('seq', 'head'), may hold values from 0 to 1
- decay_rate: float32 [128], P('head'), may hold values from 0.5 to 2
- skip: float32 [128], P('head'), may hold values from 0.5 to 1.5
- conv_x: bfloat16 [4, 8192], P(None, 'head'), may hold values from -3 to 3
- conv_bc: bfloat16 [4, 2, 1024], P(None, None, 'head'), may hold values from -3 to 3
- norm_gain: float32 [8192], P('head'), may hold values from 0.1 to 1.9
- queries: bfloat16 [24576, 2048], P(('seq', 'head')), may hold values from -9 to 9
- keys_values: bfloat16 [24576, 2, 512], P(('seq', 'head')), may hold values from -9 to 9
- doc_lengths: int32 [16], replicated, may hold values from 1 to 3072, 24576 in all
Outputs:
- mamba_out: bfloat16 [24576, 8192], P('seq', 'head')
- attn_out: bfloat16 [24576, 2048], P('seq', 'head')
The draws below stay inside these ranges and needn't reach their ends.
All inputs are finite; a program needn't handle non-finite values.
Results may differ from the reference program's by a relative error of at most 0.007.
Values may be sent and summed in bfloat16 or wider, within the bound.
A program may use at most 192 MiB of HBM per device.

```python
import math
import jax
import jax.numpy as jnp
import numpy as np
from jax import lax

TOK_DEV = 384
HEADS = 128
HEAD_DIM = 64
STATE = 128
GROUPS = 8
KW = 4
Q_HEADS = 16
KV_HEADS = 4
ATT_DIM = 128
DOCS = 16
INNER = 8192
SPAN_POSITIONS = 24576
MOST_DOC = 3072


def draw_step_size(key, part):
    key = jax.random.fold_in(key, 11)
    seed_for_forgetting, seed_for_displacement, attended_tile_sequence, attended_segment_length = jax.random.split(key, 4)
    upper = math.log(1.0 / 30.0)
    lower = math.log(0.1 / MOST_DOC)
    channelwise_forgetting = jnp.exp(jax.random.uniform(seed_for_forgetting, (HEADS,), jnp.float32, lower, upper))
    sampled_displacement = jax.random.uniform(seed_for_displacement, (SPAN_POSITIONS, HEADS), jnp.float32, 0.5, 1.5)
    block_scale = jnp.exp(jax.random.uniform(attended_tile_sequence, (SPAN_POSITIONS // TOK_DEV, 1), jnp.float32, -0.7, 0.7))
    entry_numbers = jnp.repeat(block_scale, TOK_DEV, axis=0)
    segment_lengths_choice = (jax.random.uniform(attended_segment_length, (SPAN_POSITIONS, 1), jnp.float32) < 6.0 / SPAN_POSITIONS).astype(jnp.float32)
    return (channelwise_forgetting[None, :] * sampled_displacement * entry_numbers + 0.5 * segment_lengths_choice).astype(jnp.float32)


def draw_keys_values(key, part):
    key = jax.random.fold_in(key, 21)
    normal_values = jax.random.normal(key, (SPAN_POSITIONS, 2, KV_HEADS * ATT_DIM), jnp.float32)
    return jnp.clip(normal_values, -4.0, 4.0).astype(jnp.bfloat16)


def draw_queries(key, part):
    key = jax.random.fold_in(key, 31)
    normal_values = jax.random.normal(key, (SPAN_POSITIONS, Q_HEADS * ATT_DIM), jnp.float32)
    return jnp.clip(normal_values, -4.0, 4.0).astype(jnp.bfloat16)


def levels(own_key, shape, cuts, smallest, largest):
    factor_of = 1.0
    for position, blocks in cuts:
        heights = jax.random.uniform(jax.random.fold_in(jax.random.fold_in(own_key, 6), position), (blocks,), jnp.float32, smallest / len(cuts), largest / len(cuts))
        factor_of = factor_of * jnp.repeat(jnp.exp(heights), shape[position] // blocks).reshape((-1,) + (1,) * (len(shape) - 1 - position))
    return factor_of


def profile(amount, total, reach, lean):
    portions = [(1 << 20) // math.isqrt(grade ** lean) + 1 for grade in range(2, amount + 1)]
    spare, counts = total - reach - (amount - 1), [1] * (amount - 1)
    while spare > 0:
        candidates = [i for i in range(amount - 1) if counts[i] < reach]
        pool, budget = sum([portions[i] for i in candidates]), spare
        for i in candidates:
            extra = min(reach - counts[i], max(1, budget * portions[i] // pool), spare)
            counts[i] = counts[i] + extra
            spare = spare - extra
    return np.array([reach] + counts)


def ragged(stream_key, number_of, total, reach, lean):
    if number_of == 2:
        one = jax.random.randint(stream_key, (), max(1, total - reach), min(reach, total - 1) + 1)
        return jnp.stack([one, total - one])
    sizes = jnp.asarray(profile(number_of, total, reach, lean), jnp.int32)
    couples = (number_of - 1) // 2
    donor, sink = sizes[1:1 + 2 * couples:2], sizes[2:2 + 2 * couples:2]
    slack = jnp.minimum(donor - 1, reach - sink)
    passed = jax.random.randint(jax.random.fold_in(stream_key, 1), (couples,), 0, 1 << 20) % (slack + 1)
    sizes = sizes.at[1:1 + 2 * couples:2].set(donor - passed).at[2:2 + 2 * couples:2].set(sink + passed)
    return sizes[jax.random.permutation(jax.random.fold_in(stream_key, 2), number_of)]


def gaussian(rng, extent, width, limit, pieces=(), kind=jnp.bfloat16):
    drawn = width * jax.random.normal(rng, extent, jnp.float32)
    if pieces:
        drawn = drawn * levels(rng, extent, pieces, -0.22, 0.18)
    return jnp.clip(drawn, -limit, limit).astype(kind)


def setup_inputs(seed: int = 0) -> dict:
    streams_of = jax.random.split(jax.random.key(seed), 13)
    x_in = gaussian(streams_of[0], (SPAN_POSITIONS, INNER), 1.0, 6.0, ((0, 64), (1, 4)))
    bc_in = gaussian(streams_of[1], (SPAN_POSITIONS, 2, GROUPS * STATE), 1.0, 6.0, ((0, 64), (2, 4)))
    gate_in = gaussian(streams_of[2], (SPAN_POSITIONS, INNER), 1.0, 6.0, ((0, 64), (1, 4)))
    step_size = draw_step_size(jax.random.fold_in(streams_of[12], 71), 0)
    decay_rate = jnp.clip(jnp.exp(math.log(2.0) - 1.3862944 * jax.random.uniform(streams_of[4], (HEADS,), jnp.float32) ** levels(streams_of[4], (HEADS,), ((0, 4),), -0.2, 0.2)), 0.5, 2.0)
    skip = jnp.clip(0.5 + 1.0 * jax.random.uniform(streams_of[5], (HEADS,), jnp.float32) ** levels(streams_of[5], (HEADS,), ((0, 4),), -0.2, 0.2), 0.5, 1.5)
    conv_x = gaussian(streams_of[6], (KW, INNER), KW ** -0.5, 3.0, ((1, 4),))
    conv_bc = gaussian(streams_of[7], (KW, 2, GROUPS * STATE), KW ** -0.5, 3.0, ((2, 4),))
    norm_gain = jnp.clip(1.0 + 0.18 * jax.random.normal(streams_of[8], (INNER,), jnp.float32), 0.1, 1.9)
    queries = draw_queries(jax.random.fold_in(streams_of[12], 71), 0)
    keys_values = draw_keys_values(jax.random.fold_in(streams_of[12], 71), 0)
    doc_lengths = ragged(streams_of[11], DOCS, SPAN_POSITIONS, MOST_DOC, 1).astype(jnp.int32)
    return dict(x_in=x_in, bc_in=bc_in, gate_in=gate_in, step_size=step_size, decay_rate=decay_rate, skip=skip, conv_x=conv_x, conv_bc=conv_bc, norm_gain=norm_gain, queries=queries, keys_values=keys_values, doc_lengths=doc_lengths)


EPSILON = 1e-05
NEGATIVE = -1e+30

def doc_index(positions, doc_lengths):
    doc_ends = jnp.cumsum(doc_lengths)
    return lax.optimization_barrier(jnp.sum((doc_ends[None, :] <= positions[:, None]).astype(jnp.int32), axis=1))

def convolve(values, weight, doc_ids):
    total_rows, channels = values.shape
    as_float = values.astype(jnp.float32)
    summed = jnp.zeros((total_rows, channels), jnp.float32)
    for tap_lag in range(KW):
        shifted = jnp.concatenate([jnp.zeros((tap_lag, channels), jnp.float32), as_float[:total_rows - tap_lag]], 0)
        keep_tap = jnp.concatenate([jnp.zeros((tap_lag,), bool), doc_ids[tap_lag:] == doc_ids[:total_rows - tap_lag]])
        summed = summed + jnp.where(keep_tap[:, None], shifted, 0.0) * weight[KW - 1 - tap_lag].astype(jnp.float32)
    return jax.nn.silu(summed).astype(jnp.bfloat16)

def block_terms(x_heads, b_rows, c_rows, step_rows, decay_rates, doc_ids, open_start):
    length = x_heads.shape[0]
    running = jnp.cumsum(-decay_rates[None] * step_rows, axis=0)
    row_order = jnp.arange(length, dtype=jnp.int32)
    allowed = (doc_ids[:, None] == doc_ids[None, :]) & (row_order[None, :] <= row_order[:, None])
    intersection = jnp.einsum('tgn,sgn->gts', c_rows.astype(jnp.float32), b_rows.astype(jnp.float32))
    cum_heads = jnp.moveaxis(running, 0, -1)
    log_gap = cum_heads[..., :, None] - cum_heads[..., None, :]
    decays = jnp.where(allowed, jnp.exp(jnp.where(allowed, log_gap, 0.0)), 0.0)
    mixing = decays * intersection[:, None] * jnp.moveaxis(step_rows, 0, -1)[..., None, :]
    x_float = x_heads.astype(jnp.float32)
    inner_part = jnp.einsum('ghts,sghp->tghp', mixing, x_float, precision=lax.Precision.HIGHEST)
    last_doc = doc_ids == doc_ids[-1]
    end_weight = jnp.where(last_doc[:, None, None], jnp.exp(running[-1][None] - running), 0.0) * step_rows
    end_state = jnp.einsum('sghp,sgn->ghpn', end_weight[..., None] * x_float, b_rows.astype(jnp.float32), precision=lax.Precision.HIGHEST)
    first_doc = open_start & (doc_ids == doc_ids[0])
    entry_decay = jnp.where(first_doc[:, None, None], jnp.exp(running), 0.0)
    carry_decay = jnp.where(open_start & (doc_ids[-1] == doc_ids[0]), jnp.exp(running[-1]), 0.0)
    return (inner_part, end_state, entry_decay, carry_decay, x_float)

def reference(x_in, bc_in, gate_in, step_size, decay_rate, skip, conv_x, conv_bc, norm_gain, queries, keys_values, doc_lengths):
    positions = jnp.arange(SPAN_POSITIONS, dtype=jnp.int32)
    doc_ids = doc_index(positions, doc_lengths)
    per_group = HEADS // GROUPS
    conv_inner = convolve(x_in, conv_x, doc_ids)
    conv_state = convolve(bc_in.reshape(SPAN_POSITIONS, -1), conv_bc.reshape(KW, -1), doc_ids).reshape(SPAN_POSITIONS, 2, GROUPS, STATE)
    x_heads = conv_inner.reshape(SPAN_POSITIONS, GROUPS, per_group, HEAD_DIM)
    step_heads = step_size.reshape(SPAN_POSITIONS, GROUPS, per_group)
    rate_heads = decay_rate.reshape(GROUPS, per_group)
    skip_heads = skip.reshape(GROUPS, per_group)
    blocks = SPAN_POSITIONS // TOK_DEV

    def advance(state, block_id):
        first_row = block_id * TOK_DEV

        def window_of(array):
            return lax.dynamic_slice_in_dim(array, first_row, TOK_DEV, 0)
        doc_block = window_of(doc_ids)
        prior_doc = doc_index(jnp.reshape(first_row - 1, (1,)).astype(jnp.int32), doc_lengths)[0]
        open_start = (first_row > 0) & (prior_doc == doc_block[0])
        state_block = window_of(conv_state)
        c_block = state_block[:, 1]
        inner_part, end_state, entry_decay, carry_decay, x_float = block_terms(window_of(x_heads), state_block[:, 0], c_block, window_of(step_heads), rate_heads, doc_block, open_start)
        cross = jnp.einsum('tgn,ghpn->tghp', c_block.astype(jnp.float32), state, precision=lax.Precision.HIGHEST)
        mixed = inner_part + entry_decay[..., None] * cross + skip_heads[None, :, :, None] * x_float
        new_state = carry_decay[..., None, None] * state + end_state
        return (new_state, mixed)
    start_state = jnp.zeros((GROUPS, per_group, HEAD_DIM, STATE), jnp.float32)
    _, mixed_all = lax.scan(advance, start_state, jnp.arange(blocks, dtype=jnp.int32))
    mixed_all = mixed_all.reshape(SPAN_POSITIONS, GROUPS, per_group * HEAD_DIM)
    gated = mixed_all * jax.nn.silu(gate_in.astype(jnp.float32)).reshape(SPAN_POSITIONS, GROUPS, -1)
    norm_scale = lax.rsqrt(lax.optimization_barrier(jnp.mean(gated * gated, axis=-1, keepdims=True)) + EPSILON)
    mamba_out = ((gated * norm_scale).reshape(SPAN_POSITIONS, INNER) * norm_gain).astype(jnp.bfloat16)
    group_size = Q_HEADS // KV_HEADS
    query_rows = queries.reshape(SPAN_POSITIONS, KV_HEADS, group_size, ATT_DIM)
    key_pad = jnp.zeros((MOST_DOC, KV_HEADS, ATT_DIM), jnp.bfloat16)
    key_rows = jnp.concatenate([key_pad, keys_values[:, 0].reshape(SPAN_POSITIONS, KV_HEADS, ATT_DIM)], 0)
    value_rows = jnp.concatenate([key_pad, keys_values[:, 1].reshape(SPAN_POSITIONS, KV_HEADS, ATT_DIM)], 0)
    doc_padded = jnp.concatenate([jnp.zeros((MOST_DOC,), jnp.int32) - 1, doc_ids])
    score_scale = ATT_DIM ** (-0.5)

    def attend_block(block_id):
        first_row = block_id * TOK_DEV
        span = MOST_DOC + TOK_DEV
        query_block = lax.dynamic_slice_in_dim(query_rows, first_row, TOK_DEV, 0)
        key_block = lax.dynamic_slice_in_dim(key_rows, first_row, span, 0)
        value_block = lax.dynamic_slice_in_dim(value_rows, first_row, span, 0)
        key_doc = lax.dynamic_slice_in_dim(doc_padded, first_row, span, 0)
        query_doc = lax.dynamic_slice_in_dim(doc_ids, first_row, TOK_DEV, 0)
        key_pos = first_row - MOST_DOC + jnp.arange(span, dtype=jnp.int32)
        query_pos = first_row + jnp.arange(TOK_DEV, dtype=jnp.int32)
        allowed = (query_doc[:, None] == key_doc[None, :]) & (key_pos[None, :] <= query_pos[:, None])
        scores = jnp.einsum('tkgd,skd->kgts', query_block.astype(jnp.float32), key_block.astype(jnp.float32)) * score_scale
        scores = jnp.where(allowed, scores, NEGATIVE)
        row_top = lax.optimization_barrier(jnp.max(scores, axis=-1, keepdims=True))
        weights = jnp.where(allowed, jnp.exp(scores - row_top), 0.0)
        summed = lax.optimization_barrier(jnp.sum(weights, axis=-1))
        rounded = lax.optimization_barrier(weights.astype(jnp.bfloat16)).astype(jnp.float32)
        attended = jnp.einsum('kgts,skd->kgtd', rounded, value_block.astype(jnp.float32)) / summed[..., None]
        return jnp.transpose(attended, (2, 0, 1, 3)).reshape(TOK_DEV, Q_HEADS * ATT_DIM).astype(jnp.bfloat16)
    attn_out = lax.map(attend_block, jnp.arange(blocks, dtype=jnp.int32)).reshape(SPAN_POSITIONS, Q_HEADS * ATT_DIM)
    return (mamba_out, attn_out)
```

```python
import functools
import jax
import jax.numpy as jnp
from jax import lax
from jax.experimental import pallas as pl
from jax.experimental.pallas import tpu as pltpu
from jax.sharding import PartitionSpec as P

T = 384
CH = 64
NC = T // CH
HD = 64
ST = 128
NH = 32
GC = 1024
INNER = 2 * GC
AD = 128
QH = 4
DOCS = 16
HALO = 16
BLOCKS = 64
EPSILON = 1e-05
MASKED = -1e30
SCORE = 1.4426950408889634 / AD**0.5
MESH = pl.DeviceIdType.MESH
F32 = jnp.float32
BF16 = jnp.bfloat16

Z, XP, XM, RP, RM = range(5)


def mm(a, b):
    return jnp.dot(a, b, preferred_element_type=F32)


def mm_nt(a, b):
    return lax.dot_general(a, b, (((1,), (1,)), ((), ())), preferred_element_type=F32)


def silu(v):
    half = 0.5 * v
    return half + half * jnp.tanh(half)


def split_rows(v):
    lane = lax.broadcasted_iota(jnp.int32, v.shape, 1)
    v = jnp.where(lane < NH, v, 0.0)
    high = v.astype(BF16).astype(F32)
    return (high + pltpu.roll(v - high, NH, 1)).astype(BF16)


def kernel(
    dl_ref, dec_ref, skip_ref, cx_ref, cbc_ref, gain_ref,
    x_ref, bc_ref, gate_ref, step_ref, q_ref, kv_ref,
    mo_ref, ao_ref,
    xb, bcb, gb, stt, qb, qa, kvb, cf, start, masks, xc, xs, bm, cc, ex, cum, cumd, hp, sdev, srecv, sb, tin,
    uhl, ehl, rows_sc, rex, yg, eg, ob, ab, sc, pb, mrow, lrow, arow, acc,
    loc_s, a_s, a_r, halo_s, halo_r, kv_s, kv_r, sh_s, st_s, st_r, sx_s, sx_r, tx_s, tx_r, out_s,
):
    s = lax.axis_index("seq")
    h = lax.axis_index("head")
    core = lax.rem(s, 2)
    x = lax.rem(s // 2, 4)
    z = s // 8
    first_row = s * T

    def at(zz, xx, cc_):
        return {"seq": (zz * 4 + xx) * 2 + cc_, "head": h}

    nz = lax.axis_size("seq") // 8
    z_next, z_prev = lax.rem(z + 1, nz), lax.rem(z + nz - 1, nz)
    x_next, x_prev = lax.rem(x + 1, 4), lax.rem(x + 3, 4)
    sibling = at(z, x, 1 - core)
    above, below = at(z_next, x, core), at(z_prev, x, core)
    right, left = at(z, x_next, core), at(z, x_prev, core)
    after = {"seq": lax.rem(s + 1, nz * 8), "head": h}
    before = {"seq": lax.rem(s + nz * 8 - 1, nz * 8), "head": h}

    def peer(o):
        return lax.rem(h + o, 4)

    def remote(src, dst, ssem, rsem, target):
        return pltpu.make_async_remote_copy(
            src_ref=src, dst_ref=dst, send_sem=ssem, recv_sem=rsem, device_id=target, device_id_type=MESH
        )

    loads = [
        pltpu.make_async_copy(x_ref, xb.at[pl.ds(HALO, T)], loc_s.at[0]),
        pltpu.make_async_copy(bc_ref, bcb.at[pl.ds(HALO, T)], loc_s.at[1]),
        pltpu.make_async_copy(step_ref, stt.at[pl.ds(0, NH)], loc_s.at[2]),
        pltpu.make_async_copy(gate_ref, gb, loc_s.at[3]),
        pltpu.make_async_copy(
            q_ref.at[:, pl.ds(pl.multiple_of(h * 512, 512), 512)],
            qb.at[pl.ds(pl.multiple_of(h * 96, 32), 96)], loc_s.at[4]),
        pltpu.make_async_copy(
            kv_ref.at[:, pl.ds(pl.multiple_of(h * 256, 256), 256)],
            kvb.at[0, pl.ds(pl.multiple_of(h * 96, 32), 96), pl.ds(0, 256)], loc_s.at[5]),
    ]
    for copy in loads:
        copy.start()

    barrier = pltpu.get_barrier_semaphore()
    for o in (1, 2, 3):
        pl.semaphore_signal(barrier, inc=1, device_id={"seq": s, "head": peer(o)}, device_id_type=MESH)
    for target in (before, sibling, below, left, right):
        pl.semaphore_signal(barrier, inc=1, device_id=target, device_id_type=MESH)
    pl.semaphore_wait(barrier, 8)

    def a2a(o, which):
        to = peer(o)
        target = {"seq": s, "head": to}
        mine = pl.ds(pl.multiple_of(h * 96, 32), 96)
        if which == 0:
            return remote(
                kv_ref.at[:, pl.ds(pl.multiple_of(to * 256, 256), 256)], kvb.at[0, mine, pl.ds(0, 256)],
                a_s.at[0, o - 1], a_r.at[0, o - 1], target)
        return remote(
            q_ref.at[:, pl.ds(pl.multiple_of(to * 512, 512), 512)], qb.at[mine],
            a_s.at[1, o - 1], a_r.at[1, o - 1], target)

    halo_x = remote(x_ref.at[pl.ds(T - HALO, HALO)], xb.at[pl.ds(0, HALO)], halo_s.at[0], halo_r.at[0], after)
    halo_bc = remote(bc_ref.at[pl.ds(T - HALO, HALO)], bcb.at[pl.ds(0, HALO)], halo_s.at[1], halo_r.at[1], after)
    halo_x.start()
    halo_bc.start()
    exchange = [[a2a(o, w) for o in (1, 2, 3)] for w in (0, 1)]
    for group in exchange:
        for copy in group:
            copy.start()

    def relay(buf, ssem, rsem, stride):
        def slot(d):
            return buf(d * stride)

        def copy(src, dst, k, target):
            return remote(slot(src), slot(dst), ssem.at[k], rsem.at[dst - 1], target)

        up = copy(0, 4, Z, above)
        right_own, right_far = copy(0, 1, XP, right), copy(4, 1, XP, right)
        left_own, left_far = copy(0, 3, XM, left), copy(4, 3, XM, left)
        hop_right, hop_left = copy(1, 2, RP, right), copy(3, 2, RM, left)
        inner = (x == 1) | (x == 2)

        def start_own():
            up.start()
            pl.when(x < 3)(right_own.start)
            pl.when(x == 0)(left_own.start)

        def arrived_4():
            up.wait_recv()
            pl.when(x == 3)(right_far.start)
            pl.when(x > 0)(left_far.start)

        def arrived_1():
            right_own.wait_recv()
            pl.when(inner)(hop_right.start)

        def arrived_3():
            left_own.wait_recv()
            pl.when(inner)(hop_left.start)

        def arrived_2():
            hop_right.wait_recv()

        def sent():
            up.wait_send()
            right_own.wait_send()
            left_own.wait_send()

            @pl.when(inner)
            def _():
                hop_right.wait_send()
                hop_left.wait_send()

        return start_own, arrived_4, arrived_1, arrived_3, arrived_2, sent

    kv_own, kv_4, kv_1, kv_3, kv_2, kv_sent = relay(lambda d: kvb.at[d, :, pl.ds(0, 256)], kv_s, kv_r, 2)
    st_own, st_4, st_1, st_3, st_2, st_sent = relay(lambda d: sb.at[d], st_s, st_r, 1)

    def share(i):
        return remote(
            kvb.at[2 * (i + core), :, pl.ds(0, 256)], kvb.at[2 * i + 1, :, pl.ds(0, 256)],
            sh_s.at[i], kv_r.at[4 + i], sibling)

    def share_slot(d):
        if d == 0:
            pl.when(core == 0)(share(0).start)
        elif d == 8:
            pl.when(core == 1)(share(3).start)
        else:
            for c in (0, 1):
                pl.when(core == c)(share(d // 2 - c).start)

    ends, total = [], jnp.int32(0)
    for i in range(DOCS):
        total = total + dl_ref[i]
        ends.append(total)
    row = lax.broadcasted_iota(jnp.int32, (T, 128), 0)
    lane = lax.broadcasted_iota(jnp.int32, (T, 128), 1)
    pos = row + first_row
    begin = jnp.zeros((T, 128), jnp.int32)
    for i in range(DOCS):
        begin = jnp.where(ends[i] <= pos, ends[i], begin)
    start[...] = begin
    inside = pos - begin
    for lag in (1, 2, 3):
        masks[lag - 1] = jnp.where(inside >= lag, 1.0, 0.0)
    lane1 = lax.broadcasted_iota(jnp.int32, (1, 128), 1)
    doc_first = jnp.full((1, 128), 1 << 30, jnp.int32)
    doc_end = jnp.full((1, 128), 1 << 30, jnp.int32)
    for i in range(DOCS):
        doc_end = jnp.where(lane1 == i, ends[i], doc_end)
        doc_first = jnp.where(lane1 == i, ends[i - 1] if i else 0, doc_first)
    for d in range(9):
        block = lax.rem(s + BLOCKS - d, BLOCKS)
        key = row + block * T
        hot = (key >= doc_first) & (key < doc_end)
        kvb[d, :, pl.ds(256, 128)] = jnp.where(hot, 1.0, 0.0).astype(BF16)
        if d == 0:
            blind = jnp.where(hot | (lane >= DOCS), 0.0, MASKED).astype(BF16)
            for i in range(QH):
                qa[i, :, pl.ds(128, 128)] = blind

    def expand_body(n, carry):
        r = lax.broadcasted_iota(jnp.int32, (128, 256), 0)
        c = lax.broadcasted_iota(jnp.int32, (128, 256), 1) + n * 256
        ex[:, pl.ds(pl.multiple_of(n * 256, 256), 256)] = jnp.where(
            (r < 2 * NH) & (lax.rem(r, NH) == c // HD), 1.0, 0.0).astype(BF16)
        return carry

    lax.fori_loop(0, INNER // 256, expand_body, 0)

    rows_sc[...] = jnp.zeros_like(rows_sc)
    rows_sc[pl.ds(32, 1), pl.ds(0, NH)] = dec_ref[...].reshape(1, NH)
    rows_sc[pl.ds(25, 1), pl.ds(0, NH)] = skip_ref[...].reshape(1, NH)
    loads[2].wait()
    stt[pl.ds(NH, 128 - NH)] = jnp.zeros((128 - NH, T), F32)
    step = jnp.transpose(stt[...])
    a = -(step * rows_sc[pl.ds(32, 1), :])
    a1 = a.astype(BF16).astype(F32)
    a2 = (a - a1).astype(BF16).astype(F32)
    a3 = a - a1 - a2
    parts = (a1 + pltpu.roll(a2, 32, 1) + pltpu.roll(a3, 64, 1)).astype(BF16)
    tr = lax.broadcasted_iota(jnp.int32, (T, T), 0)
    tc = lax.broadcasted_iota(jnp.int32, (T, T), 1)
    tri = jnp.where(tc <= tr, 1.0, 0.0)
    tri_ch = jnp.where((tc <= tr) & (tc // CH == tr // CH), 1.0, 0.0)

    def collect(t):
        v = mm(t.astype(BF16), parts)
        v = v + pltpu.roll(v, 96, 1) + pltpu.roll(v, 64, 1)
        return jnp.where(lane < NH, v, 0.0)

    cum[...] = collect(tri_ch)
    cumd[...] = collect(tri)
    for c in range(NC):
        rc = pl.ds(c * CH, CH)
        cu = cum[rc, :]
        mid = cum[pl.ds(c * CH + CH // 2 - 1, 1), :]
        end = cum[pl.ds(c * CH + CH - 1, 1), :]
        uhl[rc, :] = split_rows(jnp.exp(cu - mid))
        through = jnp.where(start[pl.ds(c * CH + CH - 1, 1), :] < first_row + c * CH, 1.0, 0.0)
        rows_sc[pl.ds(c, 1), :] = jnp.exp(mid)
        rows_sc[pl.ds(8 + c, 1), :] = jnp.exp(end - mid)
        rows_sc[pl.ds(16 + c, 1), :] = jnp.exp(end) * through
        cum[rc, :] = step[c * CH : (c + 1) * CH] * jnp.exp(mid - cu)
    open_dev = jnp.where(start[pl.ds(T - 1, 1), :] < first_row, 1.0, 0.0)
    rows_sc[pl.ds(24, 1), :] = jnp.exp(cumd[pl.ds(T - 1, 1), :]) * open_dev
    ehl[...] = split_rows(jnp.where(start[...] < first_row, jnp.exp(cumd[...]), 0.0))
    rex[...] = mm(split_rows(rows_sc[pl.ds(0, 32), :]), ex[...])
    svhl = split_rows(cum[...])

    loads[0].wait()
    loads[1].wait()
    halo_x.wait_recv()
    halo_bc.wait_recv()

    def convolve(src, cols, weight):
        cf[...] = src[:, cols].astype(F32)
        out = cf[pl.ds(HALO, T), :] * weight[3:4]
        for lag in (1, 2, 3):
            out = out + cf[pl.ds(HALO - lag, T), :] * masks[lag - 1] * weight[3 - lag : 4 - lag]
        return silu(out).astype(BF16)

    def conv_bc(n, carry):
        cols = pl.ds(pl.multiple_of(n * 128, 128), 128)
        out = convolve(bcb, cols, cbc_ref[:, cols].astype(F32))

        @pl.when(n < 2)
        def _():
            bm[:, cols] = out

        @pl.when(n >= 2)
        def _():
            cc[:, pl.ds(pl.multiple_of(n * 128 - 256, 128), 128)] = out
        return carry

    lax.fori_loop(0, 4, conv_bc, 0)

    def conv_x(n, carry):
        cols = pl.ds(pl.multiple_of(n * 128, 128), 128)
        out = convolve(xb, cols, cx_ref[:, cols].astype(F32))
        xc[:, cols] = out
        xs[:, cols] = (out.astype(F32) * mm(svhl, ex[:, cols])).astype(BF16)
        return carry

    lax.fori_loop(0, 16, conv_x, 0)

    loads[5].wait()
    for copy in exchange[0]:
        copy.wait_recv()
    kv_own()
    share_slot(0)

    def states(n, carry):
        cols = pl.ds(pl.multiple_of(n * 256, 256), 256)
        g = n // 4
        gl = pl.ds(pl.multiple_of(g * 128, 128), 128)
        gcols = pl.ds(pl.multiple_of(lax.rem(n, 4) * 256, 256), 256)
        state = jnp.zeros((ST, 256), F32)
        for c in range(NC):
            rc = pl.ds(c * CH, CH)
            hp[c, :, cols] = (state * rex[pl.ds(c, 1), cols]).astype(BF16)
            last = start[pl.ds(c * CH + CH - 1, 1), :]
            b = jnp.where(pos[c * CH : (c + 1) * CH] >= last, bm[rc, gl].astype(F32), 0.0).astype(BF16)
            new = lax.dot_general(b, xs[rc, cols], (((0,), (0,)), ((), ())), preferred_element_type=F32)
            state = state * rex[pl.ds(16 + c, 1), cols] + new * rex[pl.ds(8 + c, 1), cols]
        sdev[g, pl.ds(0, ST), gcols] = state.astype(BF16)
        d = jnp.broadcast_to(rex[pl.ds(24, 1), cols], (8, 256))
        high = d.astype(BF16).astype(F32)
        sdev[g, pl.ds(ST, 16), gcols] = jnp.concatenate([high, d - high], 0).astype(BF16)
        return carry

    lax.fori_loop(0, 8, states, 0)
    swap = remote(sdev.at[1 - core], srecv, sx_s, sx_r, sibling)
    swap.start()

    def decay_of(ref, cols):
        d = ref[pl.ds(ST, 16), cols].astype(F32)
        return d[0:1] + d[8:9]

    def both(cols):
        mine, other = sdev.at[core], srecv
        sm, so = mine[pl.ds(0, ST), cols].astype(F32), other[pl.ds(0, ST), cols].astype(F32)
        dm, do = decay_of(mine, cols), decay_of(other, cols)
        first = core == 0
        return (jnp.where(first, sm, so), jnp.where(first, dm, do), jnp.where(first, so, sm), jnp.where(first, do, dm))

    loads[4].wait()
    for copy in exchange[1]:
        copy.wait_recv()
    for i in range(QH):
        qa[i, :, pl.ds(0, 128)] = qb[:, pl.ds(i * 128, 128)]

    swap.wait_recv()

    def chip_state(n, carry):
        cols = pl.ds(pl.multiple_of(n * 256, 256), 256)
        s0, d0, s1, d1 = both(cols)
        sb[0, pl.ds(0, ST), cols] = (s0 * d1 + s1).astype(BF16)
        d = jnp.broadcast_to(d0 * d1, (8, 256))
        high = d.astype(BF16).astype(F32)
        sb[0, pl.ds(ST, 16), cols] = jnp.concatenate([high, d - high], 0).astype(BF16)
        return carry

    lax.fori_loop(0, 4, chip_state, 0)
    st_own()

    RT = 64

    def attend(slots, first):
        width = T * len(slots)

        def head(i, carry):
            for n, d in enumerate(slots):
                sc[:, pl.ds(n * T, T)] = mm_nt(qa[i], kvb[d, :, pl.ds(128, 256)])

            def tile(r, carry):
                rs = pl.ds(pl.multiple_of(r * RT, RT), RT)
                v = sc[rs, pl.ds(0, width)]
                if first:
                    rr = lax.broadcasted_iota(jnp.int32, (RT, T), 0) + r * RT
                    rc = lax.broadcasted_iota(jnp.int32, (RT, T), 1)
                    own = jnp.where(rc <= rr, v[:, :T], MASKED)
                    v = own if width == T else jnp.concatenate([own, v[:, T:]], 1)
                top = jnp.max(v, axis=1, keepdims=True)
                if not first:
                    old = mrow[i, rs, :]
                    new = jnp.maximum(old, top)
                    fade = jnp.exp2((old - new) * SCORE)
                    arow[rs, :] = fade
                    top = new[:, 0:1]
                else:
                    new = jnp.broadcast_to(top, (RT, 128))
                mrow[i, rs, :] = new
                p = jnp.exp2((v - top) * SCORE)
                part = p[:, 0:128]
                for k in range(1, width // 128):
                    part = part + p[:, k * 128 : (k + 1) * 128]
                lrow[i, rs, :] = part if first else lrow[i, rs, :] * fade + part
                pb[rs, pl.ds(0, width)] = p.astype(BF16)
                return carry

            lax.fori_loop(0, T // RT, tile, 0)
            out = mm(pb[:, pl.ds(0, T)], kvb[slots[0], :, pl.ds(0, 128)])
            for n, d in enumerate(slots[1:]):
                out = out + mm(pb[:, pl.ds((n + 1) * T, T)], kvb[d, :, pl.ds(0, 128)])
            acc[i] = out if first else acc[i] * arow[...] + out
            return carry

        lax.fori_loop(0, QH, head, 0)

    attend((0,), True)

    loads[3].wait()

    def local(k, carry):
        c, g = k // 2, lax.rem(k, 2)
        rc = pl.ds(pl.multiple_of(c * CH, CH), CH)
        gl = pl.ds(pl.multiple_of(g * 128, 128), 128)
        begin = start[rc, :]
        base = first_row + c * CH
        tpos = lax.broadcasted_iota(jnp.int32, (CH, CH), 0)
        spos = lax.broadcasted_iota(jnp.int32, (CH, CH), 1)
        cg = cc[rc, gl]
        grid = mm_nt(cg, bm[rc, gl])
        grid = jnp.where((spos <= tpos) & (spos + base >= begin[:, :CH]), grid, 0.0).astype(BF16)
        open_c = jnp.where(begin < base, cg.astype(F32), 0.0).astype(BF16)
        u, e = uhl[rc, :], ehl[rc, :]
        for n in range(4):
            cols = pl.ds(pl.multiple_of(g * GC + n * 256, 256), 256)
            y = mm(grid, xs[rc, cols]) + mm(open_c, hp[c, :, cols])
            y = y * mm(u, ex[:, cols]) + rex[pl.ds(25, 1), cols] * xc[rc, cols].astype(F32)
            sg = silu(gb[rc, cols].astype(F32))
            yg[rc, cols] = y * sg
            eg[rc, cols] = mm(e, ex[:, cols]) * sg
        return carry

    def locals_(lo, hi):
        lax.fori_loop(lo, hi, local, 0)

    locals_(0, 4)
    kv_4()
    share_slot(8)
    kv_1()
    share_slot(2)
    kv_3()
    share_slot(6)
    locals_(4, 8)
    st_4()
    locals_(8, 12)

    def kv_odd(i):
        share(i).wait_recv()

    kv_odd(0)
    attend((1, 2, 8), False)
    kv_2()
    share_slot(4)
    st_1()
    st_3()
    kv_odd(1)
    kv_odd(3)
    attend((3, 6, 7), False)
    kv_odd(2)
    attend((4, 5), False)

    def finish_head(i, carry):
        total = jnp.sum(lrow[i], axis=1, keepdims=True)
        ab[:, pl.ds(pl.multiple_of(i * 128, 128), 128)] = (acc[i] / total).astype(BF16)
        return carry

    lax.fori_loop(0, QH, finish_head, 0)
    out_a = pltpu.make_async_copy(ab, ao_ref, out_s.at[0])
    out_a.start()

    st_2()

    def enter(n, carry):
        cols = pl.ds(pl.multiple_of(n * 256, 256), 256)
        t = sb[4, pl.ds(0, ST), cols].astype(F32)
        for d in (3, 2, 1):
            t = sb[d, pl.ds(0, ST), cols].astype(F32) + decay_of(sb.at[d], cols) * t
        s0, d0, _, _ = both(cols)
        t1 = s0 + d0 * t
        first = core == 0
        tin[core, :, cols] = jnp.where(first, t, t1).astype(BF16)
        srecv2[:, cols] = jnp.where(first, t1, t).astype(BF16)
        return carry

    srecv2 = hp.at[0, :, pl.ds(0, GC)]
    lax.fori_loop(0, 4, enter, 0)
    give = remote(srecv2, tin.at[core], tx_s, tx_r, sibling)
    give.start()
    remote(srecv2, tin.at[1 - core], tx_s, tx_r, sibling).wait_recv()

    def tail(k, carry):
        c, g = k // 2, lax.rem(k, 2)
        rc = pl.ds(pl.multiple_of(c * CH, CH), CH)
        gl = pl.ds(pl.multiple_of(g * 128, 128), 128)
        gcols = pl.ds(pl.multiple_of(g * GC, GC), GC)
        gated = yg[rc, gcols] + eg[rc, gcols] * mm(cc[rc, gl], tin[g])
        mean = jnp.sum(gated * gated, axis=1, keepdims=True) * (1.0 / GC)
        scale = lax.rsqrt(mean + EPSILON)
        ob[rc, gcols] = (gated * scale * gain_ref[gcols].reshape(1, GC)).astype(BF16)
        pltpu.make_async_copy(ob.at[rc, gcols], mo_ref.at[rc, gcols], out_s.at[1]).start()
        return carry

    lax.fori_loop(0, 2 * NC, tail, 0)

    for group in exchange:
        for copy in group:
            copy.wait_send()
    halo_x.wait_send()
    halo_bc.wait_send()
    kv_sent()
    st_sent()
    for i in range(4):
        share(i).wait_send()
    swap.wait_send()
    give.wait_send()
    out_a.wait()
    pltpu.make_async_copy(ob, mo_ref, out_s.at[1]).wait()


def per_device(
    x_in, bc_in, gate_in, step_size, decay_rate, skip, conv_x, conv_bc, norm_gain, queries, keys_values, doc_lengths
):
    bc = bc_in.reshape(T, 512)
    cbc = conv_bc.reshape(4, 512)
    kv = jnp.stack(
        [keys_values[:, 1].reshape(96, 4, AD), keys_values[:, 0].reshape(96, 4, AD)], axis=2
    ).reshape(96, 1024)
    vm, hbm = pl.BlockSpec(memory_space=pltpu.VMEM), pl.BlockSpec(memory_space=pl.ANY)
    dma = pltpu.SemaphoreType.DMA
    V = pltpu.VMEM
    return pl.pallas_call(
        kernel,
        out_shape=(jax.ShapeDtypeStruct((T, INNER), BF16), jax.ShapeDtypeStruct((T, QH * AD), BF16)),
        in_specs=[pl.BlockSpec(memory_space=pltpu.SMEM)] + [vm] * 5 + [hbm] * 6,
        out_specs=(hbm, hbm),
        scratch_shapes=[
            V((HALO + T, INNER), BF16),
            V((HALO + T, 512), BF16),
            V((T, INNER), BF16),
            V((128, T), F32),
            V((T, 512), BF16),
            V((QH, T, 256), BF16),
            V((9, T, 384), BF16),
            V((HALO + T, 128), F32),
            V((T, 128), jnp.int32),
            V((3, T, 128), F32),
            V((T, INNER), BF16),
            V((T, INNER), BF16),
            V((T, 256), BF16),
            V((T, 256), BF16),
            V((128, INNER), BF16),
            V((T, 128), F32),
            V((T, 128), F32),
            V((NC, ST, INNER), BF16),
            V((2, ST + 16, GC), BF16),
            V((ST + 16, GC), BF16),
            V((5, ST + 16, GC), BF16),
            V((2, ST, GC), BF16),
            V((T, 128), BF16),
            V((T, 128), BF16),
            V((40, 128), F32),
            V((32, INNER), F32),
            V((T, INNER), F32),
            V((T, INNER), F32),
            V((T, INNER), BF16),
            V((T, 512), BF16),
            V((T, 3 * T), F32),
            V((T, 3 * T), BF16),
            V((QH, T, 128), F32),
            V((QH, T, 128), F32),
            V((T, 128), F32),
            V((QH, T, 128), F32),
            dma((6,)),
            dma((2, 3)),
            dma((2, 3)),
            dma((2,)),
            dma((2,)),
            dma((5,)),
            dma((8,)),
            dma((4,)),
            dma((5,)),
            dma((4,)),
            dma,
            dma,
            dma,
            dma,
            dma((2,)),
        ],
        compiler_params=pltpu.CompilerParams(
            collective_id=0, has_side_effects=True, vmem_limit_bytes=60 * 1024 * 1024
        ),
        name="hybrid",
    )(doc_lengths, decay_rate, skip, conv_x, cbc, norm_gain, x_in, bc, gate_in, step_size.T, queries, kv)


def solution(mesh):
    placed = (
        P("seq", "head"),
        P("seq", None, "head"),
        P("seq", "head"),
        P("seq", "head"),
        P("head"),
        P("head"),
        P(None, "head"),
        P(None, None, "head"),
        P("head"),
        P(("seq", "head"), None),
        P(("seq", "head"), None, None),
        P(),
    )
    return jax.shard_map(
        per_device,
        mesh=mesh,
        in_specs=placed,
        out_specs=(P("seq", "head"), P("seq", "head")),
        check_vma=False,
    )
```

```python
import functools
import jax
import jax.numpy as jnp
from jax import lax
from jax.experimental import pallas as pl
from jax.experimental.pallas import tpu as pltpu
from jax.sharding import PartitionSpec as P

T = 384
CH = 64
NC = T // CH
HD = 64
ST = 128
NH = 32
GC = 1024
INNER = 2 * GC
AD = 128
QH = 4
DOCS = 16
HALO = 16
BLOCKS = 64
EPSILON = 1e-05
MASKED = -1e30
SCORE = 1.4426950408889634 / AD**0.5
MESH = pl.DeviceIdType.MESH
F32 = jnp.float32
BF16 = jnp.bfloat16

Z, XP, XM, RP, RM = range(5)


def mm(a, b):
    return jnp.dot(a, b, preferred_element_type=F32)


def mm_nt(a, b):
    return lax.dot_general(a, b, (((1,), (1,)), ((), ())), preferred_element_type=F32)


def silu(v):
    half = 0.5 * v
    return half + half * jnp.tanh(half)


def split_rows(v):
    lane = lax.broadcasted_iota(jnp.int32, v.shape, 1)
    v = jnp.where(lane < NH, v, 0.0)
    high = v.astype(BF16).astype(F32)
    return (high + pltpu.roll(v - high, NH, 1)).astype(BF16)


def kernel(
    dl_ref, dec_ref, skip_ref, cx_ref, cbc_ref,
    x_ref, bc_ref, gate_ref, step_ref, q_ref, kv_ref,
    yg_ref, eg_ref, cc_ref, tin_ref, ao_ref,
    xb, bc3, bcb, cbc, gb, stt, qb, qa, kv3, kvb, cf, start, masks, xc, xs, bm, cc, ex, cum, cumd, hp, sdev, srecv, sb, tin,
    uhl, ehl, rows_sc, rex, yg, eg, ab, sc0, sc1, pb0, pb1, mrow, lrow, ar0, ar1, acc,
    loc_s, a_s, a_r, halo_s, halo_r, kv_s, kv_r, sh_s, st_s, st_r, sx_s, sx_r, tx_s, tx_r, out_s,
):
    s = lax.axis_index("seq")
    h = lax.axis_index("head")
    core = lax.rem(s, 2)
    x = lax.rem(s // 2, 4)
    z = s // 8
    first_row = s * T

    def at(zz, xx, cc_):
        return {"seq": (zz * 4 + xx) * 2 + cc_, "head": h}

    nz = lax.axis_size("seq") // 8
    z_next, z_prev = lax.rem(z + 1, nz), lax.rem(z + nz - 1, nz)
    x_next, x_prev = lax.rem(x + 1, 4), lax.rem(x + 3, 4)
    sibling = at(z, x, 1 - core)
    above, below = at(z_next, x, core), at(z_prev, x, core)
    right, left = at(z, x_next, core), at(z, x_prev, core)
    after = {"seq": lax.rem(s + 1, nz * 8), "head": h}
    before = {"seq": lax.rem(s + nz * 8 - 1, nz * 8), "head": h}

    def peer(o):
        return lax.rem(h + o, 4)

    def remote(src, dst, ssem, rsem, target):
        return pltpu.make_async_remote_copy(
            src_ref=src, dst_ref=dst, send_sem=ssem, recv_sem=rsem, device_id=target, device_id_type=MESH
        )

    loads = [
        pltpu.make_async_copy(x_ref, xb.at[pl.ds(HALO, T)], loc_s.at[0]),
        pltpu.make_async_copy(bc_ref, bc3.at[pl.ds(HALO, T)], loc_s.at[1]),
        pltpu.make_async_copy(step_ref, stt.at[pl.ds(0, NH)], loc_s.at[2]),
        pltpu.make_async_copy(gate_ref, gb, loc_s.at[3]),
        pltpu.make_async_copy(
            q_ref.at[:, pl.ds(pl.multiple_of(h * 512, 512), 512)],
            qb.at[pl.ds(pl.multiple_of(h * 96, 32), 96)], loc_s.at[4]),
        pltpu.make_async_copy(
            kv_ref.at[:, :, pl.ds(pl.multiple_of(h * 128, 128), 128)],
            kv3.at[pl.ds(pl.multiple_of(h * 96, 32), 96)], loc_s.at[5]),
    ]
    for copy in loads:
        copy.start()

    barrier = pltpu.get_barrier_semaphore()
    for o in (1, 2, 3):
        pl.semaphore_signal(barrier, inc=1, device_id={"seq": s, "head": peer(o)}, device_id_type=MESH)
    for target in (before, sibling, below, left, right):
        pl.semaphore_signal(barrier, inc=1, device_id=target, device_id_type=MESH)
    pl.semaphore_wait(barrier, 8)

    def a2a(o, which):
        to = peer(o)
        target = {"seq": s, "head": to}
        mine = pl.ds(pl.multiple_of(h * 96, 32), 96)
        if which == 0:
            return remote(
                kv_ref.at[:, :, pl.ds(pl.multiple_of(to * 128, 128), 128)], kv3.at[mine],
                a_s.at[0, o - 1], a_r.at[0, o - 1], target)
        return remote(
            q_ref.at[:, pl.ds(pl.multiple_of(to * 512, 512), 512)], qb.at[mine],
            a_s.at[1, o - 1], a_r.at[1, o - 1], target)

    halo_x = remote(x_ref.at[pl.ds(T - HALO, HALO)], xb.at[pl.ds(0, HALO)], halo_s.at[0], halo_r.at[0], after)
    halo_bc = remote(bc_ref.at[pl.ds(T - HALO, HALO)], bc3.at[pl.ds(0, HALO)], halo_s.at[1], halo_r.at[1], after)
    halo_x.start()
    halo_bc.start()
    exchange = [[a2a(o, w) for o in (1, 2, 3)] for w in (0, 1)]
    for copy in exchange[0]:
        copy.start()

    def relay(buf, ssem, rsem, stride):
        def slot(d):
            return buf(d * stride)

        def copy(src, dst, k, target):
            return remote(slot(src), slot(dst), ssem.at[k], rsem.at[dst - 1], target)

        up = copy(0, 4, Z, above)
        right_own, right_far = copy(0, 1, XP, right), copy(4, 1, XP, right)
        left_own, left_far = copy(0, 3, XM, left), copy(4, 3, XM, left)
        hop_right, hop_left = copy(1, 2, RP, right), copy(3, 2, RM, left)
        inner = (x == 1) | (x == 2)

        def start_own():
            up.start()
            pl.when(x < 3)(right_own.start)
            pl.when(x == 0)(left_own.start)

        def arrived_4():
            up.wait_recv()
            pl.when(x == 3)(right_far.start)
            pl.when(x > 0)(left_far.start)

        def arrived_1():
            right_own.wait_recv()
            pl.when(inner)(hop_right.start)

        def arrived_3():
            left_own.wait_recv()
            pl.when(inner)(hop_left.start)

        def arrived_2():
            hop_right.wait_recv()

        def sent():
            up.wait_send()
            right_own.wait_send()
            left_own.wait_send()

            @pl.when(inner)
            def _():
                hop_right.wait_send()
                hop_left.wait_send()

        return start_own, arrived_4, arrived_1, arrived_3, arrived_2, sent

    kv_own, kv_4, kv_1, kv_3, kv_2, kv_sent = relay(lambda d: kvb.at[d, :, pl.ds(0, 256)], kv_s, kv_r, 2)
    st_own, st_4, st_1, st_3, st_2, st_sent = relay(lambda d: sb.at[d], st_s, st_r, 1)

    def share(i):
        return remote(
            kvb.at[2 * (i + core), :, pl.ds(0, 256)], kvb.at[2 * i + 1, :, pl.ds(0, 256)],
            sh_s.at[i], kv_r.at[4 + i], sibling)

    def share_slot(d):
        if d == 0:
            pl.when(core == 0)(share(0).start)
        elif d == 8:
            pl.when(core == 1)(share(3).start)
        else:
            for c in (0, 1):
                pl.when(core == c)(share(d // 2 - c).start)

    ends, total = [], jnp.int32(0)
    for i in range(DOCS):
        total = total + dl_ref[i]
        ends.append(total)
    row = lax.broadcasted_iota(jnp.int32, (T, 128), 0)
    lane = lax.broadcasted_iota(jnp.int32, (T, 128), 1)
    pos = row + first_row
    begin = jnp.zeros((T, 128), jnp.int32)
    for i in range(DOCS):
        begin = jnp.where(ends[i] <= pos, ends[i], begin)
    start[...] = begin
    inside = pos - begin
    for lag in (1, 2, 3):
        masks[lag - 1] = jnp.where(inside >= lag, 1.0, 0.0)
    lane1 = lax.broadcasted_iota(jnp.int32, (1, 128), 1)
    doc_first = jnp.full((1, 128), 1 << 30, jnp.int32)
    doc_end = jnp.full((1, 128), 1 << 30, jnp.int32)
    for i in range(DOCS):
        doc_end = jnp.where(lane1 == i, ends[i], doc_end)
        doc_first = jnp.where(lane1 == i, ends[i - 1] if i else 0, doc_first)
    for d in range(9):
        block = lax.rem(s + BLOCKS - d, BLOCKS)
        key = row + block * T
        hot = (key >= doc_first) & (key < doc_end)
        kvb[d, :, pl.ds(256, 128)] = jnp.where(hot, 1.0, 0.0).astype(BF16)
        if d == 0:
            blind = jnp.where(hot | (lane >= DOCS), 0.0, MASKED).astype(BF16)
            for i in range(QH):
                qa[i, :, pl.ds(128, 128)] = blind

    def expand_body(n, carry):
        r = lax.broadcasted_iota(jnp.int32, (128, 256), 0)
        c = lax.broadcasted_iota(jnp.int32, (128, 256), 1) + n * 256
        ex[:, pl.ds(pl.multiple_of(n * 256, 256), 256)] = jnp.where(
            (r < 2 * NH) & (lax.rem(r, NH) == c // HD), 1.0, 0.0).astype(BF16)
        return carry

    lax.fori_loop(0, INNER // 256, expand_body, 0)

    rows_sc[...] = jnp.zeros_like(rows_sc)
    rows_sc[pl.ds(32, 1), pl.ds(0, NH)] = dec_ref[...].reshape(1, NH)
    rows_sc[pl.ds(25, 1), pl.ds(0, NH)] = skip_ref[...].reshape(1, NH)
    loads[2].wait()
    stt[pl.ds(NH, 128 - NH)] = jnp.zeros((128 - NH, T), F32)
    step = jnp.transpose(stt[...])
    a = -(step * rows_sc[pl.ds(32, 1), :])
    a1 = a.astype(BF16).astype(F32)
    a2 = (a - a1).astype(BF16).astype(F32)
    a3 = a - a1 - a2
    parts = (a1 + pltpu.roll(a2, 32, 1) + pltpu.roll(a3, 64, 1)).astype(BF16)
    tr = lax.broadcasted_iota(jnp.int32, (T, T), 0)
    tc = lax.broadcasted_iota(jnp.int32, (T, T), 1)
    tri = jnp.where(tc <= tr, 1.0, 0.0)
    tri_ch = jnp.where((tc <= tr) & (tc // CH == tr // CH), 1.0, 0.0)

    def collect(t):
        v = mm(t.astype(BF16), parts)
        v = v + pltpu.roll(v, 96, 1) + pltpu.roll(v, 64, 1)
        return jnp.where(lane < NH, v, 0.0)

    cum[...] = collect(tri_ch)
    cumd[...] = collect(tri)
    for c in range(NC):
        rc = pl.ds(c * CH, CH)
        cu = cum[rc, :]
        mid = cum[pl.ds(c * CH + CH // 2 - 1, 1), :]
        end = cum[pl.ds(c * CH + CH - 1, 1), :]
        uhl[rc, :] = split_rows(jnp.exp(cu - mid))
        through = jnp.where(start[pl.ds(c * CH + CH - 1, 1), :] < first_row + c * CH, 1.0, 0.0)
        rows_sc[pl.ds(c, 1), :] = jnp.exp(mid)
        rows_sc[pl.ds(8 + c, 1), :] = jnp.exp(end - mid)
        rows_sc[pl.ds(16 + c, 1), :] = jnp.exp(end) * through
        cum[rc, :] = step[c * CH : (c + 1) * CH] * jnp.exp(mid - cu)
    open_dev = jnp.where(start[pl.ds(T - 1, 1), :] < first_row, 1.0, 0.0)
    rows_sc[pl.ds(24, 1), :] = jnp.exp(cumd[pl.ds(T - 1, 1), :]) * open_dev
    ehl[...] = split_rows(jnp.where(start[...] < first_row, jnp.exp(cumd[...]), 0.0))
    rex[...] = mm(split_rows(rows_sc[pl.ds(0, 32), :]), ex[...])
    svhl = split_rows(cum[...])

    loads[0].wait()
    loads[1].wait()
    halo_x.wait_recv()
    halo_bc.wait_recv()

    split = jnp.swapaxes(bc3[...], 0, 1)
    bcb[:, pl.ds(0, 256)] = split[0]
    bcb[:, pl.ds(256, 256)] = split[1]
    taps_bc = jnp.swapaxes(cbc_ref[...], 0, 1).astype(F32)
    cbc[:, pl.ds(0, 256)] = taps_bc[0]
    cbc[:, pl.ds(256, 256)] = taps_bc[1]

    def convolve(src, cols, weight):
        cf[...] = src[:, cols].astype(F32)
        out = cf[pl.ds(HALO, T), :] * weight[3:4]
        for lag in (1, 2, 3):
            out = out + cf[pl.ds(HALO - lag, T), :] * masks[lag - 1] * weight[3 - lag : 4 - lag]
        return silu(out).astype(BF16)

    def conv_bc(n, carry):
        cols = pl.ds(pl.multiple_of(n * 128, 128), 128)
        out = convolve(bcb, cols, cbc[:, cols])

        @pl.when(n < 2)
        def _():
            bm[:, cols] = out

        @pl.when(n >= 2)
        def _():
            cc[:, pl.ds(pl.multiple_of(n * 128 - 256, 128), 128)] = out
        return carry

    lax.fori_loop(0, 4, conv_bc, 0)
    out_c = pltpu.make_async_copy(cc, cc_ref, out_s.at[3])
    out_c.start()

    def conv_x(n, carry):
        cols = pl.ds(pl.multiple_of(n * 128, 128), 128)
        out = convolve(xb, cols, cx_ref[:, cols].astype(F32))
        xc[:, cols] = out
        xs[:, cols] = (out.astype(F32) * mm(svhl, ex[:, cols])).astype(BF16)
        return carry

    lax.fori_loop(0, 8, conv_x, 0)

    loads[5].wait()
    for copy in exchange[0]:
        copy.wait_recv()
    pair = jnp.swapaxes(kv3[...], 0, 1)
    kvb[0, :, pl.ds(0, 128)] = pair[1]
    kvb[0, :, pl.ds(128, 128)] = pair[0]
    kv_own()
    share_slot(0)
    for copy in exchange[1]:
        copy.start()
    lax.fori_loop(8, 16, conv_x, 0)

    def states(n, carry):
        cols = pl.ds(pl.multiple_of(n * 256, 256), 256)
        g = n // 4
        gl = pl.ds(pl.multiple_of(g * 128, 128), 128)
        gcols = pl.ds(pl.multiple_of(lax.rem(n, 4) * 256, 256), 256)
        state = jnp.zeros((ST, 256), F32)
        for c in range(NC):
            rc = pl.ds(c * CH, CH)
            hp[c, :, cols] = (state * rex[pl.ds(c, 1), cols]).astype(BF16)
            last = start[pl.ds(c * CH + CH - 1, 1), :]
            b = jnp.where(pos[c * CH : (c + 1) * CH] >= last, bm[rc, gl].astype(F32), 0.0).astype(BF16)
            new = lax.dot_general(b, xs[rc, cols], (((0,), (0,)), ((), ())), preferred_element_type=F32)
            state = state * rex[pl.ds(16 + c, 1), cols] + new * rex[pl.ds(8 + c, 1), cols]
        sdev[g, pl.ds(0, ST), gcols] = state.astype(BF16)
        d = jnp.broadcast_to(rex[pl.ds(24, 1), cols], (8, 256))
        high = d.astype(BF16).astype(F32)
        sdev[g, pl.ds(ST, 16), gcols] = jnp.concatenate([high, d - high], 0).astype(BF16)
        return carry

    lax.fori_loop(0, 8, states, 0)
    swap = remote(sdev.at[1 - core], srecv, sx_s, sx_r, sibling)
    swap.start()

    def decay_of(ref, cols):
        d = ref[pl.ds(ST, 16), cols].astype(F32)
        return d[0:1] + d[8:9]

    def both(cols):
        mine, other = sdev.at[core], srecv
        sm, so = mine[pl.ds(0, ST), cols].astype(F32), other[pl.ds(0, ST), cols].astype(F32)
        dm, do = decay_of(mine, cols), decay_of(other, cols)
        first = core == 0
        return (jnp.where(first, sm, so), jnp.where(first, dm, do), jnp.where(first, so, sm), jnp.where(first, do, dm))

    loads[4].wait()
    for copy in exchange[1]:
        copy.wait_recv()
    for i in range(QH):
        qa[i, :, pl.ds(0, 128)] = qb[:, pl.ds(i * 128, 128)]

    swap.wait_recv()

    def chip_state(n, carry):
        cols = pl.ds(pl.multiple_of(n * 256, 256), 256)
        s0, d0, s1, d1 = both(cols)
        sb[0, pl.ds(0, ST), cols] = (s0 * d1 + s1).astype(BF16)
        d = jnp.broadcast_to(d0 * d1, (8, 256))
        high = d.astype(BF16).astype(F32)
        sb[0, pl.ds(ST, 16), cols] = jnp.concatenate([high, d - high], 0).astype(BF16)
        return carry

    lax.fori_loop(0, 4, chip_state, 0)
    st_own()

    RT = 128
    scs, pbs, ars = (sc0, sc1), (pb0, pb1), (ar0, ar1)

    def attend(slots, first):
        tiles = T * len(slots) // 128

        def scores(i):
            for n, d in enumerate(slots):
                scs[i % 2][:, pl.ds(n * T, T)] = mm_nt(qa[i], kvb[d, :, pl.ds(128, 256)])

        def block(i, r, k):
            v = scs[i % 2][pl.ds(r * RT, RT), pl.ds(k * 128, 128)]
            if first and k == r:
                rr = lax.broadcasted_iota(jnp.int32, (RT, 128), 0)
                cc_ = lax.broadcasted_iota(jnp.int32, (RT, 128), 1)
                v = jnp.where(cc_ <= rr, v, MASKED)
            return v

        def highest(i, r):
            rs = pl.ds(r * RT, RT)
            top = block(i, r, 0)
            for k in range(1, r + 1 if first else tiles):
                top = jnp.maximum(top, block(i, r, k))
            top = jnp.max(top, axis=1, keepdims=True)
            if first:
                mrow[i, rs, :] = jnp.broadcast_to(top, (RT, 128))
            else:
                old = mrow[i, rs, :]
                new = jnp.maximum(old, top)
                ars[i % 2][rs, :] = jnp.exp2((old - new) * SCORE)
                mrow[i, rs, :] = new

        def weigh(i, r):
            rs = pl.ds(r * RT, RT)
            new, part = mrow[i, rs, :], None
            for k in range(tiles):
                if first and k > r:
                    pbs[i % 2][rs, pl.ds(k * 128, 128)] = jnp.zeros((RT, 128), BF16)
                    continue
                p = jnp.exp2((block(i, r, k) - new) * SCORE)
                part = p if part is None else part + p
                pbs[i % 2][rs, pl.ds(k * 128, 128)] = p.astype(BF16)
            lrow[i, rs, :] = part if first else lrow[i, rs, :] * ars[i % 2][rs, :] + part

        def gather(i):
            out = mm(pbs[i % 2][:, pl.ds(0, T)], kvb[slots[0], :, pl.ds(0, 128)])
            for n, d in enumerate(slots[1:]):
                out = out + mm(pbs[i % 2][:, pl.ds((n + 1) * T, T)], kvb[d, :, pl.ds(0, 128)])
            acc[i] = out if first else acc[i] * ars[i % 2][...] + out

        scores(0)
        for i in range(QH):
            if i + 1 < QH:
                scores(i + 1)
            if i > 0:
                gather(i - 1)
            for r in range(T // RT):
                highest(i, r)
            for r in range(T // RT):
                weigh(i, r)
        gather(QH - 1)

    attend((0,), True)

    loads[3].wait()

    def local(k, carry):
        c, g = k // 2, lax.rem(k, 2)
        rc = pl.ds(pl.multiple_of(c * CH, CH), CH)
        gl = pl.ds(pl.multiple_of(g * 128, 128), 128)
        begin = start[rc, :]
        base = first_row + c * CH
        tpos = lax.broadcasted_iota(jnp.int32, (CH, CH), 0)
        spos = lax.broadcasted_iota(jnp.int32, (CH, CH), 1)
        cg = cc[rc, gl]
        grid = mm_nt(cg, bm[rc, gl])
        grid = jnp.where((spos <= tpos) & (spos + base >= begin[:, :CH]), grid, 0.0).astype(BF16)
        open_c = jnp.where(begin < base, cg.astype(F32), 0.0).astype(BF16)
        u, e = uhl[rc, :], ehl[rc, :]
        for n in range(4):
            cols = pl.ds(pl.multiple_of(g * GC + n * 256, 256), 256)
            y = mm(grid, xs[rc, cols]) + mm(open_c, hp[c, :, cols])
            y = y * mm(u, ex[:, cols]) + rex[pl.ds(25, 1), cols] * xc[rc, cols].astype(F32)
            sg = silu(gb[rc, cols].astype(F32))
            yg[rc, cols] = (y * sg).astype(BF16)
            eg[rc, cols] = (mm(e, ex[:, cols]) * sg).astype(BF16)
        gcols = pl.ds(pl.multiple_of(g * GC, GC), GC)
        pltpu.make_async_copy(yg.at[rc, gcols], yg_ref.at[rc, gcols], out_s.at[1]).start()
        pltpu.make_async_copy(eg.at[rc, gcols], eg_ref.at[rc, gcols], out_s.at[2]).start()
        return carry

    def locals_(lo, hi):
        lax.fori_loop(lo, hi, local, 0)

    locals_(0, 4)
    kv_4()
    share_slot(8)
    kv_1()
    share_slot(2)
    kv_3()
    share_slot(6)
    locals_(4, 8)
    st_4()
    locals_(8, 12)

    def kv_odd(i):
        share(i).wait_recv()

    kv_odd(0)
    attend((1, 2, 8), False)
    kv_2()
    share_slot(4)
    st_1()
    st_3()
    kv_odd(1)
    kv_odd(3)
    attend((3, 6, 7), False)
    kv_odd(2)
    attend((4, 5), False)

    def finish_head(i, carry):
        total = jnp.sum(lrow[i], axis=1, keepdims=True)
        ab[:, pl.ds(pl.multiple_of(i * 128, 128), 128)] = (acc[i] / total).astype(BF16)
        return carry

    lax.fori_loop(0, QH, finish_head, 0)
    out_a = pltpu.make_async_copy(ab, ao_ref, out_s.at[0])
    out_a.start()

    st_2()

    def enter(n, carry):
        cols = pl.ds(pl.multiple_of(n * 256, 256), 256)
        t = sb[4, pl.ds(0, ST), cols].astype(F32)
        for d in (3, 2, 1):
            t = sb[d, pl.ds(0, ST), cols].astype(F32) + decay_of(sb.at[d], cols) * t
        s0, d0, _, _ = both(cols)
        t1 = s0 + d0 * t
        first = core == 0
        tin[core, :, cols] = jnp.where(first, t, t1).astype(BF16)
        srecv2[:, cols] = jnp.where(first, t1, t).astype(BF16)
        return carry

    srecv2 = hp.at[0, :, pl.ds(0, GC)]
    lax.fori_loop(0, 4, enter, 0)
    give = remote(srecv2, tin.at[core], tx_s, tx_r, sibling)
    give.start()
    remote(srecv2, tin.at[1 - core], tx_s, tx_r, sibling).wait_recv()

    out_t = pltpu.make_async_copy(tin, tin_ref, out_s.at[4])
    out_t.start()
    for group in exchange:
        for copy in group:
            copy.wait_send()
    halo_x.wait_send()
    halo_bc.wait_send()
    kv_sent()
    st_sent()
    for i in range(4):
        share(i).wait_send()
    swap.wait_send()
    give.wait_send()
    out_a.wait()
    pltpu.make_async_copy(yg, yg_ref, out_s.at[1]).wait()
    pltpu.make_async_copy(eg, eg_ref, out_s.at[2]).wait()
    out_c.wait()
    out_t.wait()


TR = 64


def finish(yg_ref, eg_ref, cc_ref, tin_ref, gain_ref, a_ref, mo_ref, ao_ref, yg, eg, cc, tin, ab, ob, in_s, row_s, out_s):
    small = [
        pltpu.make_async_copy(tin_ref, tin, in_s.at[0]),
        pltpu.make_async_copy(cc_ref, cc, in_s.at[1]),
    ]
    rows = [pl.ds(i * TR, TR) for i in range(T // TR)]
    large = [
        (pltpu.make_async_copy(yg_ref.at[r], yg.at[r], row_s.at[0, i]),
         pltpu.make_async_copy(eg_ref.at[r], eg.at[r], row_s.at[1, i])) for i, r in enumerate(rows)
    ]
    attention = pltpu.make_async_copy(a_ref, ab, in_s.at[2])
    for copy in small:
        copy.start()
    for pair in large:
        for copy in pair:
            copy.start()
    attention.start()
    for copy in small:
        copy.wait()
    outs = []
    for i, r in enumerate(rows):
        for copy in large[i]:
            copy.wait()
        for g in range(2):
            cols = pl.ds(g * GC, GC)
            gated = yg[r, cols].astype(F32) + eg[r, cols].astype(F32) * mm(cc[r, pl.ds(g * 128, 128)], tin[g])
            mean = jnp.sum(gated * gated, axis=1, keepdims=True) * (1.0 / GC)
            scale = lax.rsqrt(mean + EPSILON)
            ob[r, cols] = (gated * scale * gain_ref[cols].reshape(1, GC)).astype(BF16)
        outs.append(pltpu.make_async_copy(ob.at[r], mo_ref.at[r], out_s.at[i]))
        outs[-1].start()
    attention.wait()
    outs.append(pltpu.make_async_copy(ab, ao_ref, out_s.at[T // TR]))
    outs[-1].start()
    for copy in outs:
        copy.wait()


def per_device(
    x_in, bc_in, gate_in, step_size, decay_rate, skip, conv_x, conv_bc, norm_gain, queries, keys_values, doc_lengths
):
    vm, hbm = pl.BlockSpec(memory_space=pltpu.VMEM), pl.BlockSpec(memory_space=pl.ANY)
    dma = pltpu.SemaphoreType.DMA
    V = pltpu.VMEM
    shape = jax.ShapeDtypeStruct
    main = pl.pallas_call(
        kernel,
        out_shape=(
            shape((T, INNER), BF16), shape((T, INNER), BF16), shape((T, 256), BF16),
            shape((2, ST, GC), BF16), shape((T, QH * AD), BF16),
        ),
        in_specs=[pl.BlockSpec(memory_space=pltpu.SMEM)] + [vm] * 4 + [hbm] * 6,
        out_specs=(hbm,) * 5,
        scratch_shapes=[
            V((HALO + T, INNER), BF16),
            V((HALO + T, 2, 256), BF16),
            V((HALO + T, 512), BF16),
            V((4, 512), F32),
            V((T, INNER), BF16),
            V((128, T), F32),
            V((T, 512), BF16),
            V((QH, T, 256), BF16),
            V((T, 2, 128), BF16),
            V((9, T, 384), BF16),
            V((HALO + T, 128), F32),
            V((T, 128), jnp.int32),
            V((3, T, 128), F32),
            V((T, INNER), BF16),
            V((T, INNER), BF16),
            V((T, 256), BF16),
            V((T, 256), BF16),
            V((128, INNER), BF16),
            V((T, 128), F32),
            V((T, 128), F32),
            V((NC, ST, INNER), BF16),
            V((2, ST + 16, GC), BF16),
            V((ST + 16, GC), BF16),
            V((5, ST + 16, GC), BF16),
            V((2, ST, GC), BF16),
            V((T, 128), BF16),
            V((T, 128), BF16),
            V((40, 128), F32),
            V((32, INNER), F32),
            V((T, INNER), BF16),
            V((T, INNER), BF16),
            V((T, 512), BF16),
            V((T, 3 * T), F32),
            V((T, 3 * T), F32),
            V((T, 3 * T), BF16),
            V((T, 3 * T), BF16),
            V((QH, T, 128), F32),
            V((QH, T, 128), F32),
            V((T, 128), F32),
            V((T, 128), F32),
            V((QH, T, 128), F32),
            dma((6,)),
            dma((2, 3)),
            dma((2, 3)),
            dma((2,)),
            dma((2,)),
            dma((5,)),
            dma((8,)),
            dma((4,)),
            dma((5,)),
            dma((4,)),
            dma,
            dma,
            dma,
            dma,
            dma((5,)),
        ],
        compiler_params=pltpu.CompilerParams(
            collective_id=0, has_side_effects=True, vmem_limit_bytes=60 * 1024 * 1024
        ),
        name="hybrid",
    )
    yg, eg, cc, tin, attended = main(
        doc_lengths, decay_rate, skip, conv_x, conv_bc, x_in, bc_in, gate_in, step_size.T, queries, keys_values)
    return pl.pallas_call(
        finish,
        out_shape=(shape((T, INNER), BF16), shape((T, QH * AD), BF16)),
        in_specs=[hbm] * 4 + [vm, hbm],
        out_specs=(hbm, hbm),
        scratch_shapes=[
            V((T, INNER), BF16), V((T, INNER), BF16), V((T, 256), BF16), V((2, ST, GC), BF16),
            V((T, QH * AD), BF16), V((T, INNER), BF16),
            dma((3,)), dma((2, T // TR)), dma((T // TR + 1,)),
        ],
        compiler_params=pltpu.CompilerParams(vmem_limit_bytes=60 * 1024 * 1024),
        name="finish",
    )(yg, eg, cc, tin, norm_gain, attended)


def solution(mesh):
    placed = (
        P("seq", "head"),
        P("seq", None, "head"),
        P("seq", "head"),
        P("seq", "head"),
        P("head"),
        P("head"),
        P(None, "head"),
        P(None, None, "head"),
        P("head"),
        P(("seq", "head"), None),
        P(("seq", "head"), None, None),
        P(),
    )
    return jax.shard_map(
        per_device,
        mesh=mesh,
        in_specs=placed,
        out_specs=(P("seq", "head"), P("seq", "head")),
        check_vma=False,
    )
```

```python
import functools
import jax
import jax.numpy as jnp
from jax import lax
from jax.experimental import pallas as pl
from jax.experimental.pallas import tpu as pltpu
from jax.sharding import PartitionSpec as P

T = 384
CH = 64
NC = T // CH
HD = 64
ST = 128
NH = 32
GC = 1024
INNER = 2 * GC
AD = 128
QH = 4
DOCS = 16
HALO = 16
BLOCKS = 64
EPSILON = 1e-05
MASKED = -1e30
SCORE = 1.4426950408889634 / AD**0.5
MESH = pl.DeviceIdType.MESH
F32 = jnp.float32
BF16 = jnp.bfloat16
HT = T // 2
NQ = GC // 4


def mm(a, b):
    return jnp.dot(a, b, preferred_element_type=F32)


def mm_nt(a, b):
    return lax.dot_general(a, b, (((1,), (1,)), ((), ())), preferred_element_type=F32)


def silu(v):
    half = 0.5 * v
    return half + half * jnp.tanh(half)


def split_rows(v):
    lane = lax.broadcasted_iota(jnp.int32, v.shape, 1)
    v = jnp.where(lane < NH, v, 0.0)
    high = v.astype(BF16).astype(F32)
    return (high + pltpu.roll(v - high, NH, 1)).astype(BF16)


def kernel(
    dl_ref, dec_ref, skip_ref, cx_ref, cbc_ref,
    x_ref, bc_ref, gate_ref, step_ref, q_ref, kv_ref,
    yg_ref, eg_ref, cc_ref, tin_ref, ao_ref,
    xb, hx, bc3, hb3, bcb, cbc, gb, stt, qb, qa, kv3, kvb, cf0, cf1, start, masks, xc, xh, fixed, fixed_s, bm, bt, mix, ex, cum, cumd, sdev, srecv, sq, got, tq, tback, give_b, tin,
    uhl, ehl, rows_sc, rex, ue, ee, yg, eg, cc, ab, sc0, sc1, pb0, pb1, mrow, lrow, ar0, ar1, acc,
    loc_s, a_s, a_r, halo_s, halo_r, z_s, z_r, row_s, row_r, sh_s, sh_r, st_s, st_r, tq_s, tq_r,
    sx_s, sx_r, tx_s, tx_r, out_s,
):
    s = lax.axis_index("seq")
    h = lax.axis_index("head")
    core = lax.rem(s, 2)
    x = lax.rem(s // 2, 4)
    z = s // 8
    first_row = s * T

    def at(zz, xx, cc_):
        return {"seq": (zz * 4 + xx) * 2 + cc_, "head": h}

    nz = lax.axis_size("seq") // 8
    z_next, z_prev = lax.rem(z + 1, nz), lax.rem(z + nz - 1, nz)
    right = [lax.rem(x + o, 4) for o in range(4)]
    left = [lax.rem(x + 4 - o, 4) for o in range(4)]
    sibling = at(z, x, 1 - core)
    above = at(z_next, x, core)
    after = {"seq": lax.rem(s + 1, nz * 8), "head": h}
    before = {"seq": lax.rem(s + nz * 8 - 1, nz * 8), "head": h}

    def peer(o):
        return lax.rem(h + o, 4)

    def remote(src, dst, ssem, rsem, target):
        return pltpu.make_async_remote_copy(
            src_ref=src, dst_ref=dst, send_sem=ssem, recv_sem=rsem, device_id=target, device_id_type=MESH
        )

    loads = [
        pltpu.make_async_copy(x_ref, xb.at[pl.ds(HALO, T)], loc_s.at[0]),
        pltpu.make_async_copy(bc_ref, bc3, loc_s.at[1]),
        pltpu.make_async_copy(step_ref, stt.at[pl.ds(0, NH)], loc_s.at[2]),
        pltpu.make_async_copy(gate_ref, gb, loc_s.at[3]),
        pltpu.make_async_copy(
            q_ref.at[:, pl.ds(pl.multiple_of(h * 512, 512), 512)],
            qb.at[pl.ds(pl.multiple_of(h * 96, 32), 96)], loc_s.at[4]),
        pltpu.make_async_copy(
            kv_ref.at[:, :, pl.ds(pl.multiple_of(h * 128, 128), 128)],
            kv3.at[pl.ds(pl.multiple_of(h * 96, 32), 96)], loc_s.at[5]),
    ]
    for copy in loads:
        copy.start()

    barrier = pltpu.get_barrier_semaphore()
    for o in (1, 2, 3):
        pl.semaphore_signal(barrier, inc=1, device_id={"seq": s, "head": peer(o)}, device_id_type=MESH)
    for target in (before, sibling):
        pl.semaphore_signal(barrier, inc=1, device_id=target, device_id_type=MESH)
    for o in (1, 2, 3):
        pl.semaphore_signal(barrier, inc=1, device_id=at(z, left[o], core), device_id_type=MESH)
    for o in (0, 1, 2, 3):
        pl.semaphore_signal(barrier, inc=1, device_id=at(z_prev, left[o], core), device_id_type=MESH)

    def a2a(o, which):
        to = peer(o)
        target = {"seq": s, "head": to}
        mine = pl.ds(pl.multiple_of(h * 96, 32), 96)
        if which == 0:
            return remote(
                kv_ref.at[:, :, pl.ds(pl.multiple_of(to * 128, 128), 128)], kv3.at[mine],
                a_s.at[0, o - 1], a_r.at[0, o - 1], target)
        return remote(
            q_ref.at[:, pl.ds(pl.multiple_of(to * 512, 512), 512)], qb.at[mine],
            a_s.at[1, o - 1], a_r.at[1, o - 1], target)

    halo_x = remote(x_ref.at[pl.ds(T - HALO, HALO)], hx, halo_s.at[0], halo_r.at[0], after)
    halo_bc = remote(bc_ref.at[pl.ds(T - HALO, HALO)], hb3, halo_s.at[1], halo_r.at[1], after)
    exchange = [[a2a(o, w) for o in (1, 2, 3)] for w in (0, 1)]

    def block_half(d, i):
        return kvb.at[d, pl.ds(i * HT, HT), pl.ds(0, 256)]

    rise = [remote(block_half(0, i), block_half(8, i), z_s.at[i], z_r.at[i], above) for i in (0, 1)]

    def along(o, i, source):
        return remote(
            block_half(source, i), block_half(2 * o, i), row_s.at[o - 1, i], row_r.at[o - 1, i], at(z, right[o], core))

    def kv_own():
        for copy in rise:
            copy.start()
        for o in (1, 2, 3):
            @pl.when(x + o < 4)
            def _():
                for i in (0, 1):
                    along(o, i, 0).start()

    def kv_risen(i):
        rise[i].wait_recv()
        for o in (3, 2, 1):
            pl.when(x + o >= 4)(along(o, i, 8).start)

    def kv_row(o):
        for i in (0, 1):
            along(o, i, 0).wait_recv()

    def share(i):
        return remote(
            kvb.at[2 * (i + core), :, pl.ds(0, 256)], kvb.at[2 * i + 1, :, pl.ds(0, 256)],
            sh_s.at[i], sh_r.at[i], sibling)

    def share_slot(d):
        if d == 0:
            pl.when(core == 0)(share(0).start)
        elif d == 8:
            pl.when(core == 1)(share(3).start)
        else:
            for c in (0, 1):
                pl.when(core == c)(share(d // 2 - c).start)

    def shared(d):
        if d in (0, 8):
            pl.when(core == 1)(share(0).wait_recv)
            pl.when(core == 0)(share(3).wait_recv)
        else:
            for c in (0, 1):
                pl.when(core == c)(share(d // 2 - 1 + c).wait_recv)

    ends, total = [], jnp.int32(0)
    for i in range(DOCS):
        total = total + dl_ref[i]
        ends.append(total)
    row = lax.broadcasted_iota(jnp.int32, (T, 128), 0)
    lane = lax.broadcasted_iota(jnp.int32, (T, 128), 1)
    pos = row + first_row
    begin = jnp.zeros((T, 128), jnp.int32)
    for i in range(DOCS):
        begin = jnp.where(ends[i] <= pos, ends[i], begin)
    start[...] = begin
    inside = pos - begin
    for lag in (1, 2, 3):
        masks[lag - 1] = jnp.where(inside >= lag, 1.0, 0.0)
    lane1 = lax.broadcasted_iota(jnp.int32, (1, 128), 1)
    doc_first = jnp.full((1, 128), 1 << 30, jnp.int32)
    doc_end = jnp.full((1, 128), 1 << 30, jnp.int32)
    for i in range(DOCS):
        doc_end = jnp.where(lane1 == i, ends[i], doc_end)
        doc_first = jnp.where(lane1 == i, ends[i - 1] if i else 0, doc_first)
    def expand_body(n, carry):
        r = lax.broadcasted_iota(jnp.int32, (128, 256), 0)
        c = lax.broadcasted_iota(jnp.int32, (128, 256), 1) + n * 256
        ex[:, pl.ds(pl.multiple_of(n * 256, 256), 256)] = jnp.where(
            (r < 2 * NH) & ((r & (NH - 1)) == (c >> 6)), 1.0, 0.0).astype(BF16)
        return carry

    lax.fori_loop(0, INNER // 256, expand_body, 0)

    rows_sc[...] = jnp.zeros_like(rows_sc)
    rows_sc[pl.ds(32, 1), pl.ds(0, NH)] = dec_ref[...].reshape(1, NH)
    rows_sc[pl.ds(25, 1), pl.ds(0, NH)] = skip_ref[...].reshape(1, NH)
    loads[2].wait()
    stt[pl.ds(NH, 128 - NH)] = jnp.zeros((128 - NH, T), F32)
    step = jnp.transpose(stt[...])
    a = -(step * rows_sc[pl.ds(32, 1), :])
    a1 = a.astype(BF16).astype(F32)
    a2 = (a - a1).astype(BF16).astype(F32)
    a3 = a - a1 - a2
    parts = (a1 + pltpu.roll(a2, 32, 1) + pltpu.roll(a3, 64, 1)).astype(BF16)
    tr = lax.broadcasted_iota(jnp.int32, (T, T), 0)
    tc = lax.broadcasted_iota(jnp.int32, (T, T), 1)
    tri = jnp.where(tc <= tr, 1.0, 0.0)
    tri_ch = jnp.where((tc <= tr) & ((tc >> 6) == (tr >> 6)), 1.0, 0.0)

    def collect(t):
        v = mm(t.astype(BF16), parts)
        v = v + pltpu.roll(v, 96, 1) + pltpu.roll(v, 64, 1)
        return jnp.where(lane < NH, v, 0.0)

    cum[...] = collect(tri_ch)
    cumd[...] = collect(tri)
    for c in range(NC):
        rc = pl.ds(c * CH, CH)
        cu = cum[rc, :]
        mid = cum[pl.ds(c * CH + CH // 2 - 1, 1), :]
        end = cum[pl.ds(c * CH + CH - 1, 1), :]
        uhl[rc, :] = split_rows(jnp.exp(cu - mid))
        through = jnp.where(start[pl.ds(c * CH + CH - 1, 1), :] < first_row + c * CH, 1.0, 0.0)
        rows_sc[pl.ds(c, 1), :] = jnp.exp(mid)
        rows_sc[pl.ds(8 + c, 1), :] = jnp.exp(end - mid)
        rows_sc[pl.ds(16 + c, 1), :] = jnp.exp(end) * through
        cum[rc, :] = step[c * CH : (c + 1) * CH] * jnp.exp(mid - cu)
    open_dev = jnp.where(start[pl.ds(T - 1, 1), :] < first_row, 1.0, 0.0)
    rows_sc[pl.ds(24, 1), :] = jnp.exp(cumd[pl.ds(T - 1, 1), :]) * open_dev
    ehl[...] = split_rows(jnp.where(start[...] < first_row, jnp.exp(cumd[...]), 0.0))
    rex[...] = mm(split_rows(rows_sc[pl.ds(0, 32), :]), ex[...])
    svhl = split_rows(cum[...])

    pl.semaphore_wait(barrier, 12)
    halo_x.start()
    halo_bc.start()
    for copy in exchange[0]:
        copy.start()

    loads[0].wait()
    loads[1].wait()
    xb[pl.ds(0, HALO), :] = jnp.zeros((HALO, INNER), BF16)
    bcb[pl.ds(0, HALO), :] = jnp.zeros((HALO, 512), BF16)
    split = jnp.swapaxes(bc3[...], 0, 1)
    bcb[pl.ds(HALO, T), pl.ds(0, 256)] = split[0]
    bcb[pl.ds(HALO, T), pl.ds(256, 256)] = split[1]
    taps_bc = jnp.swapaxes(cbc_ref[...], 0, 1).astype(F32)
    cbc[:, pl.ds(0, 256)] = taps_bc[0]
    cbc[:, pl.ds(256, 256)] = taps_bc[1]

    def convolve(src, cols, weight, cf):
        cf[...] = src[:, cols].astype(F32)
        out = cf[pl.ds(HALO, T), :] * weight[3:4]
        for lag in (1, 2, 3):
            out = out + cf[pl.ds(HALO - lag, T), :] * masks[lag - 1] * weight[3 - lag : 4 - lag]
        return silu(out).astype(BF16)

    def conv_bc(n, carry):
        cols = pl.ds(pl.multiple_of(n * 128, 128), 128)
        out = convolve(bcb, cols, cbc[:, cols], cf0)

        @pl.when(n < 2)
        def _():
            bm[:, cols] = out

        @pl.when(n >= 2)
        def _():
            cc[:, pl.ds(pl.multiple_of(n * 128 - 256, 128), 128)] = out
        return carry

    lax.fori_loop(0, 4, conv_bc, 0)

    def conv_quarter(o):
        def body(g, carry):
            first = g * GC + right[o] * NQ
            both_cols = pl.ds(pl.multiple_of(first, NQ), NQ)
            out = []
            for k, cf in enumerate((cf0, cf1)):
                cols = pl.ds(pl.multiple_of(first + k * 128, 128), 128)
                out.append(convolve(xb, cols, cx_ref[:, cols].astype(F32), cf))
                xc[:, cols] = out[-1]
            scale = mm(svhl, ex[:, both_cols])
            for k in (0, 1):
                cols = pl.ds(pl.multiple_of(first + k * 128, 128), 128)
                scaled = (out[k].astype(F32) * scale[:, k * 128 : (k + 1) * 128]).astype(BF16)
                for c in range(NC):
                    xh[c, pl.ds(ST, CH), cols] = scaled[c * CH : (c + 1) * CH]
            return carry

        lax.fori_loop(0, 2, body, 0)

    order = (2, 1, 3, 0)

    conv_quarter(order[0])
    conv_quarter(order[1])

    loads[5].wait()
    for copy in exchange[0]:
        copy.wait_recv()
    pair = jnp.swapaxes(kv3[...], 0, 1)
    kvb[0, :, pl.ds(0, 128)] = pair[1]
    kvb[0, :, pl.ds(128, 128)] = pair[0]
    kv_own()
    share_slot(0)
    for copy in exchange[1]:
        copy.start()

    halo_x.wait_recv()
    halo_bc.wait_recv()

    def first_rows(halo, own, weight):
        width = own.shape[1]
        v = jnp.concatenate([halo, own], 0).astype(F32)
        out = v[HALO:] * weight[3:4]
        for lag in (1, 2, 3):
            mask = jnp.concatenate([masks[lag - 1, pl.ds(0, HALO), :]] * (width // 128), 1)
            out = out + pltpu.roll(v, lag, 0)[HALO:] * mask * weight[3 - lag : 4 - lag]
        return silu(out).astype(BF16)

    halo_pair = jnp.swapaxes(hb3[...], 0, 1)
    head_rows, own_rows = pl.ds(0, HALO), pl.ds(HALO, HALO)
    bm[head_rows, :] = first_rows(halo_pair[0], bcb[own_rows, pl.ds(0, 256)], cbc[:, pl.ds(0, 256)])
    cc[head_rows, :] = first_rows(halo_pair[1], bcb[own_rows, pl.ds(256, 256)], cbc[:, pl.ds(256, 256)])
    for n in range(4):
        cols = pl.ds(n * 512, 512)
        out = first_rows(hx[:, cols], xb[own_rows, cols], cx_ref[:, cols].astype(F32))
        fixed[:, cols] = out
        fixed_s[:, cols] = (out.astype(F32) * mm(svhl[:HALO], ex[:, cols])).astype(BF16)

    out_c = pltpu.make_async_copy(cc, cc_ref, out_s.at[3])
    out_c.start()

    for c in range(NC):
        last = start[pl.ds(c * CH + CH - 1, 1), :]
        reach = pos[c * CH : (c + 1) * CH] >= last
        for g in (0, 1):
            b = jnp.where(reach, bm[pl.ds(c * CH, CH), pl.ds(g * 128, 128)].astype(F32), 0.0)
            bt[g, c] = jnp.transpose(b).astype(BF16)

    def end_states(o):
        quarter = right[o]

        def body(g, carry):
            cols = pl.ds(pl.multiple_of(g * GC + quarter * NQ, NQ), NQ)
            xc[head_rows, cols] = fixed[:, cols]
            xh[0, pl.ds(ST, HALO), cols] = fixed_s[:, cols]
            state = None
            for c in range(NC):
                if c == 0:
                    xh[c, pl.ds(0, ST), cols] = jnp.zeros((ST, NQ), BF16)
                else:
                    xh[c, pl.ds(0, ST), cols] = (state * rex[pl.ds(c, 1), cols]).astype(BF16)
                new = mm(bt[g, c], xh[c, pl.ds(ST, CH), cols])
                new = new * rex[pl.ds(8 + c, 1), cols]
                state = new if c == 0 else state * rex[pl.ds(16 + c, 1), cols] + new
            sdev[g, quarter, pl.ds(0, ST), :] = state.astype(BF16)
            d = jnp.broadcast_to(rex[pl.ds(24, 1), cols], (8, NQ))
            high = d.astype(BF16).astype(F32)
            sdev[g, quarter, pl.ds(ST, 16), :] = jnp.concatenate([high, d - high], 0).astype(BF16)
            return carry

        lax.fori_loop(0, 2, body, 0)

    def swap(o):
        return remote(
            sdev.at[1 - core, right[o]], srecv.at[right[o]], sx_s.at[o], sx_r.at[o], sibling)

    def decay_of(ref):
        d = ref[pl.ds(ST, 16), :].astype(F32)
        return d[0:1] + d[8:9]

    def both(quarter):
        mine, other = sdev.at[core, quarter], srecv.at[quarter]
        sm, so = mine[pl.ds(0, ST), :].astype(F32), other[pl.ds(0, ST), :].astype(F32)
        dm, do = decay_of(mine), decay_of(other)
        first = core == 0
        return (jnp.where(first, sm, so), jnp.where(first, dm, do), jnp.where(first, so, sm), jnp.where(first, do, dm))

    def deal(o):
        copies = [remote(sq.at[right[o]], got.at[1, x], st_s.at[3 + o], st_r.at[3 + o], at(z_next, right[o], core))]
        if o:
            copies.append(
                remote(sq.at[right[o]], got.at[0, x], st_s.at[o - 1], st_r.at[o - 1], at(z, right[o], core)))
        return copies

    def chip_state(o):
        quarter = right[o]
        swap(o).wait_recv()
        s0, d0, s1, d1 = both(quarter)
        sq[quarter, pl.ds(0, ST), :] = (s0 * d1 + s1).astype(BF16)
        d = jnp.broadcast_to(d0 * d1, (8, NQ))
        high = d.astype(BF16).astype(F32)
        sq[quarter, pl.ds(ST, 16), :] = jnp.concatenate([high, d - high], 0).astype(BF16)
        for copy in deal(o):
            copy.start()

    end_states(order[0])
    swap(order[0]).start()
    end_states(order[1])
    swap(order[1]).start()
    chip_state(order[0])

    for k in (2, 3):
        conv_quarter(order[k])
        chip_state(order[k - 1])
        end_states(order[k])
        swap(order[k]).start()

    for d in range(9):
        block = lax.rem(s + BLOCKS - d, BLOCKS)
        key = row + block * T
        hot = (key >= doc_first) & (key < doc_end)
        kvb[d, :, pl.ds(256, 128)] = jnp.where(hot, 1.0, 0.0).astype(BF16)
        if d == 0:
            blind = jnp.where(hot | (lane >= DOCS), 0.0, MASKED).astype(BF16)
            for i in range(QH):
                qa[i, :, pl.ds(128, 128)] = blind

    loads[4].wait()
    for copy in exchange[1]:
        copy.wait_recv()
    for i in range(QH):
        qa[i, :, pl.ds(0, 128)] = qb[:, pl.ds(i * 128, 128)]

    chip_state(order[3])
    kv_risen(0)
    got[0, x] = sq[x]

    RT = 128
    scs, pbs, ars = (sc0, sc1), (pb0, pb1), (ar0, ar1)

    def attend(slots, first):
        tiles = T * len(slots) // 128

        def scores(i):
            for n, d in enumerate(slots):
                scs[i % 2][:, pl.ds(n * T, T)] = mm_nt(qa[i], kvb[d, :, pl.ds(128, 256)])

        def block(i, r, k):
            v = scs[i % 2][pl.ds(r * RT, RT), pl.ds(k * 128, 128)]
            if first and k == r:
                rr = lax.broadcasted_iota(jnp.int32, (RT, 128), 0)
                cc_ = lax.broadcasted_iota(jnp.int32, (RT, 128), 1)
                v = jnp.where(cc_ <= rr, v, MASKED)
            return v

        def highest(i, r):
            rs = pl.ds(r * RT, RT)
            top = block(i, r, 0)
            for k in range(1, r + 1 if first else tiles):
                top = jnp.maximum(top, block(i, r, k))
            top = jnp.max(top, axis=1, keepdims=True)
            if first:
                mrow[i, rs, :] = jnp.broadcast_to(top, (RT, 128))
            else:
                old = mrow[i, rs, :]
                new = jnp.maximum(old, top)
                ars[i % 2][rs, :] = jnp.exp2((old - new) * SCORE)
                mrow[i, rs, :] = new

        def weigh(i, r):
            rs = pl.ds(r * RT, RT)
            new, part = mrow[i, rs, :], None
            for k in range(tiles):
                if first and k > r:
                    pbs[i % 2][rs, pl.ds(k * 128, 128)] = jnp.zeros((RT, 128), BF16)
                    continue
                p = jnp.exp2((block(i, r, k) - new) * SCORE)
                part = p if part is None else part + p
                pbs[i % 2][rs, pl.ds(k * 128, 128)] = p.astype(BF16)
            lrow[i, rs, :] = part if first else lrow[i, rs, :] * ars[i % 2][rs, :] + part

        def gather(i):
            out = mm(pbs[i % 2][:, pl.ds(0, T)], kvb[slots[0], :, pl.ds(0, 128)])
            for n, d in enumerate(slots[1:]):
                out = out + mm(pbs[i % 2][:, pl.ds((n + 1) * T, T)], kvb[d, :, pl.ds(0, 128)])
            acc[i] = out if first else acc[i] * ars[i % 2][...] + out

        scores(0)
        for i in range(QH):
            if i + 1 < QH:
                scores(i + 1)
            if i > 0:
                gather(i - 1)
            for r in range(T // RT):
                highest(i, r)
            for r in range(T // RT):
                weigh(i, r)
        gather(QH - 1)

    attend((0,), True)

    loads[3].wait()

    for c in range(NC):
        rc = pl.ds(c * CH, CH)
        begin = start[rc, :]
        base = first_row + c * CH
        tpos = lax.broadcasted_iota(jnp.int32, (CH, CH), 0)
        spos = lax.broadcasted_iota(jnp.int32, (CH, CH), 1)
        for g in (0, 1):
            gl = pl.ds(g * 128, 128)
            cg = cc[rc, gl]
            grid = mm_nt(cg, bm[rc, gl])
            grid = jnp.where((spos <= tpos) & (spos + base >= begin[:, :CH]), grid, 0.0).astype(BF16)
            mix[g, c, :, pl.ds(0, 128)] = jnp.where(begin < base, cg.astype(F32), 0.0).astype(BF16)
            mix[g, c, :, pl.ds(128, CH)] = grid

    def local(n, carry):
        g = n >> 2
        cols = pl.ds(pl.multiple_of(n * 256, 256), 256)
        ue[...] = mm(uhl[...], ex[:, cols])
        ee[...] = mm(ehl[...], ex[:, cols])
        for c in range(NC):
            rc = pl.ds(c * CH, CH)
            y = mm(mix[g, c], xh[c, :, cols])
            y = y * ue[rc, :] + rex[pl.ds(25, 1), cols] * xc[rc, cols].astype(F32)
            sg = silu(gb[rc, cols].astype(F32))
            yg[rc, cols] = (y * sg).astype(BF16)
            eg[rc, cols] = (ee[rc, :] * sg).astype(BF16)
        pltpu.make_async_copy(yg.at[:, cols], yg_ref.at[:, cols], out_s.at[1]).start()
        pltpu.make_async_copy(eg.at[:, cols], eg_ref.at[:, cols], out_s.at[2]).start()
        return carry

    def locals_(lo, hi):
        lax.fori_loop(lo, hi, local, 0)

    kv_risen(1)
    share_slot(8)
    locals_(0, 4)
    shared(8)
    attend((8, 7 - 6 * core), False)

    for o in order:
        for copy in deal(o):
            copy.wait_recv()

    def decay(r, j):
        d = got[r, j, pl.ds(ST, 16), :].astype(F32)
        return d[0:1] + d[8:9]

    def entering(n, carry):
        rs = pl.ds(pl.multiple_of(n * 32, 32), 32)
        later, fall = [None] * 4, None
        for j in (3, 2, 1, 0):
            v = got[1, j, rs, :].astype(F32)
            later[j] = v if j == 3 else later[j + 1] + fall * v
            fall = decay(1, j) if j == 3 else fall * decay(1, j)
        tq[0, rs, :] = later[0].astype(BF16)
        for j in (0, 1, 2):
            v = got[0, j, rs, :].astype(F32)
            row_sum = v if j == 0 else v + decay(0, j) * row_sum
            fall = decay(0, j) if j == 0 else fall * decay(0, j)
            tq[j + 1, rs, :] = (row_sum + fall * later[j + 1]).astype(BF16)
        return carry

    lax.fori_loop(0, ST // 32, entering, 0)
    back = [
        remote(tq.at[right[o]], tback.at[x], tq_s.at[o - 1], tq_r.at[o - 1], at(z, right[o], core)) for o in (1, 2, 3)
    ]
    for copy in back:
        copy.start()
    tback[x] = tq[x]

    locals_(4, 6)
    for o in (1, 2, 3):
        kv_row(o)
        share_slot(2 * o)
    locals_(6, 8)
    shared(2)
    shared(4)
    attend((2, 1 + 2 * core, 4, 3 + 2 * core), False)
    for copy in back:
        copy.wait_recv()

    def enter(n, carry):
        cols = pl.ds(pl.multiple_of(n * NQ, NQ), NQ)
        t = tback[n].astype(F32)
        s0, d0, _, _ = both(n)
        t1 = s0 + d0 * t
        first = core == 0
        tin[core, :, cols] = jnp.where(first, t, t1).astype(BF16)
        give_b[:, cols] = jnp.where(first, t1, t).astype(BF16)
        return carry

    lax.fori_loop(0, 4, enter, 0)
    give = remote(give_b, tin.at[core], tx_s, tx_r, sibling)
    give.start()
    shared(6)
    attend((6, 5 + 2 * core), False)

    def finish_head(i, carry):
        total = jnp.sum(lrow[i], axis=1, keepdims=True)
        ab[:, pl.ds(pl.multiple_of(i * 128, 128), 128)] = (acc[i] / total).astype(BF16)
        return carry

    lax.fori_loop(0, QH, finish_head, 0)
    out_a = pltpu.make_async_copy(ab, ao_ref, out_s.at[0])
    out_a.start()

    remote(give_b, tin.at[1 - core], tx_s, tx_r, sibling).wait_recv()

    out_t = pltpu.make_async_copy(tin, tin_ref, out_s.at[4])
    out_t.start()

    for group in exchange:
        for copy in group:
            copy.wait_send()
    halo_x.wait_send()
    halo_bc.wait_send()
    for i in (0, 1):
        rise[i].wait_send()
        for o in (1, 2, 3):
            along(o, i, 0).wait_send()
    for o in order:
        swap(o).wait_send()
        for copy in deal(o):
            copy.wait_send()
    for copy in back:
        copy.wait_send()
    for i in range(4):
        share(i).wait_send()
    give.wait_send()
    out_a.wait()
    pltpu.make_async_copy(yg, yg_ref, out_s.at[1]).wait()
    pltpu.make_async_copy(eg, eg_ref, out_s.at[2]).wait()
    out_c.wait()
    out_t.wait()

TR = 128
SUB = 16


def finish(yg_ref, eg_ref, cc_ref, tin_ref, gain_ref, a_ref, mo_ref, ao_ref, yg, eg, cc, tin, ab, far, ob, in_s, row_s, out_s):
    small = [pltpu.make_async_copy(tin_ref, tin, in_s.at[0]), pltpu.make_async_copy(cc_ref, cc, in_s.at[1])]
    large = []
    for i in range(T // TR):
        r = pl.ds(i * TR, TR)
        large.append((
            pltpu.make_async_copy(yg_ref.at[r], yg.at[r], row_s.at[0, i]),
            pltpu.make_async_copy(eg_ref.at[r], eg.at[r], row_s.at[1, i])))
    came = pltpu.make_async_copy(a_ref, ab, in_s.at[2])
    for copy in small + [copy for pair in large for copy in pair] + [came]:
        copy.start()
    for copy in small:
        copy.wait()
    attention = pltpu.make_async_copy(ab, ao_ref, out_s.at[T // TR])
    outs = [attention]
    for i in range(T // TR):
        r = pl.ds(i * TR, TR)
        for copy in large[i]:
            copy.wait()
        for g in range(2):
            cols = pl.ds(g * GC, GC)
            gain = gain_ref[cols].reshape(1, GC)
            far[r, cols] = mm(cc[r, pl.ds(g * 128, 128)], tin[g])
            for k in range(TR // SUB):
                q = pl.ds(i * TR + k * SUB, SUB)
                gated = yg[q, cols].astype(F32) + eg[q, cols].astype(F32) * far[q, cols]
                mean = jnp.sum(gated * gated, axis=1, keepdims=True) * (1.0 / GC)
                scale = lax.rsqrt(mean + EPSILON)
                ob[q, cols] = (gated * scale * gain).astype(BF16)
        outs.append(pltpu.make_async_copy(ob.at[r], mo_ref.at[r], out_s.at[i]))
        outs[-1].start()
    came.wait()
    attention.start()
    for copy in outs:
        copy.wait()


def per_device(
    x_in, bc_in, gate_in, step_size, decay_rate, skip, conv_x, conv_bc, norm_gain, queries, keys_values, doc_lengths
):
    vm, hbm = pl.BlockSpec(memory_space=pltpu.VMEM), pl.BlockSpec(memory_space=pltpu.HBM)
    dma = pltpu.SemaphoreType.DMA
    V = pltpu.VMEM
    shape = jax.ShapeDtypeStruct
    main = pl.pallas_call(
        kernel,
        out_shape=(
            shape((T, INNER), BF16), shape((T, INNER), BF16), shape((T, 256), BF16),
            shape((2, ST, GC), BF16), shape((T, QH * AD), BF16),
        ),
        in_specs=[pl.BlockSpec(memory_space=pltpu.SMEM)] + [vm] * 4 + [hbm] * 6,
        out_specs=(hbm,) * 5,
        scratch_shapes=[
            V((HALO + T, INNER), BF16),
            V((HALO, INNER), BF16),
            V((T, 2, 256), BF16),
            V((HALO, 2, 256), BF16),
            V((HALO + T, 512), BF16),
            V((4, 512), F32),
            V((T, INNER), BF16),
            V((128, T), F32),
            V((T, 512), BF16),
            V((QH, T, 256), BF16),
            V((T, 2, 128), BF16),
            V((9, T, 384), BF16),
            V((HALO + T, 128), F32),
            V((HALO + T, 128), F32),
            V((T, 128), jnp.int32),
            V((3, T, 128), F32),
            V((T, INNER), BF16),
            V((NC, ST + CH, INNER), BF16),
            V((HALO, INNER), BF16),
            V((HALO, INNER), BF16),
            V((T, 256), BF16),
            V((2, NC, ST, CH), BF16),
            V((2, NC, CH, ST + CH), BF16),
            V((128, INNER), BF16),
            V((T, 128), F32),
            V((T, 128), F32),
            V((2, 4, ST + 16, NQ), BF16),
            V((4, ST + 16, NQ), BF16),
            V((4, ST + 16, NQ), BF16),
            V((2, 4, ST + 16, NQ), BF16),
            V((4, ST, NQ), BF16),
            V((4, ST, NQ), BF16),
            V((ST, GC), BF16),
            V((2, ST, GC), BF16),
            V((T, 128), BF16),
            V((T, 128), BF16),
            V((40, 128), F32),
            V((32, INNER), F32),
            V((T, 256), F32),
            V((T, 256), F32),
            V((T, INNER), BF16),
            V((T, INNER), BF16),
            V((T, 256), BF16),
            V((T, 512), BF16),
            V((T, 4 * T), F32),
            V((T, 4 * T), F32),
            V((T, 4 * T), BF16),
            V((T, 4 * T), BF16),
            V((QH, T, 128), F32),
            V((QH, T, 128), F32),
            V((T, 128), F32),
            V((T, 128), F32),
            V((QH, T, 128), F32),
            dma((6,)),
            dma((2, 3)),
            dma((2, 3)),
            dma((2,)),
            dma((2,)),
            dma((2,)),
            dma((2,)),
            dma((3, 2)),
            dma((3, 2)),
            dma((4,)),
            dma((4,)),
            dma((7,)),
            dma((7,)),
            dma((3,)),
            dma((3,)),
            dma((4,)),
            dma((4,)),
            dma,
            dma,
            dma((5,)),
        ],
        compiler_params=pltpu.CompilerParams(
            collective_id=0, has_side_effects=True, vmem_limit_bytes=60 * 1024 * 1024
        ),
        name="hybrid",
    )
    yg, eg, cc, tin, attended = main(
        doc_lengths, decay_rate, skip, conv_x, conv_bc, x_in, bc_in, gate_in, step_size.T, queries, keys_values)
    return pl.pallas_call(
        finish,
        out_shape=(shape((T, INNER), BF16), shape((T, QH * AD), BF16)),
        in_specs=[hbm] * 4 + [vm, hbm],
        out_specs=(hbm, hbm),
        scratch_shapes=[
            V((T, INNER), BF16), V((T, INNER), BF16), V((T, 256), BF16), V((2, ST, GC), BF16), V((T, QH * AD), BF16),
            V((T, INNER), F32), V((T, INNER), BF16), dma((3,)), dma((2, T // TR)), dma((T // TR + 1,)),
        ],
        compiler_params=pltpu.CompilerParams(vmem_limit_bytes=60 * 1024 * 1024),
        name="finish",
    )(yg, eg, cc, tin, norm_gain, attended)


def solution(mesh):
    placed = (
        P("seq", "head"),
        P("seq", None, "head"),
        P("seq", "head"),
        P("seq", "head"),
        P("head"),
        P("head"),
        P(None, "head"),
        P(None, None, "head"),
        P("head"),
        P(("seq", "head"), None),
        P(("seq", "head"), None, None),
        P(),
    )
    return jax.shard_map(
        per_device,
        mesh=mesh,
        in_specs=placed,
        out_specs=(P("seq", "head"), P("seq", "head")),
        check_vma=False,
    )
```

```python
import functools
import jax
import jax.numpy as jnp
from jax import lax
from jax.experimental import pallas as pl
from jax.experimental.pallas import tpu as pltpu
from jax.sharding import PartitionSpec as P

T = 384
CH = 64
NC = T // CH
HD = 64
ST = 128
NH = 32
GC = 1024
INNER = 2 * GC
AD = 128
QH = 4
DOCS = 16
HALO = 16
BLOCKS = 64
EPSILON = 1e-05
MASKED = -1e30
SCORE = 1.4426950408889634 / AD**0.5
MESH = pl.DeviceIdType.MESH
F32 = jnp.float32
BF16 = jnp.bfloat16
HT = T // 2
NQ = GC // 4


def mm(a, b):
    return jnp.dot(a, b, preferred_element_type=F32)


def mm_nt(a, b):
    return lax.dot_general(a, b, (((1,), (1,)), ((), ())), preferred_element_type=F32)


def silu(v):
    half = 0.5 * v
    return half + half * jnp.tanh(half)


def split_rows(v):
    lane = lax.broadcasted_iota(jnp.int32, v.shape, 1)
    v = jnp.where(lane < NH, v, 0.0)
    high = v.astype(BF16).astype(F32)
    return (high + pltpu.roll(v - high, NH, 1)).astype(BF16)


def kernel(
    dl_ref, dec_ref, skip_ref, cx_ref, cbc_ref,
    x_ref, bc_ref, gate_ref, step_ref, q_ref, kv_ref,
    yg_ref, eg_ref, cc_ref, tin_ref, ao_ref,
    xb, hx, bc3, hb3, bcb, cbc, gb, stt, qb, qa, kv3, kv3z, kvb, cf0, cf1, start, masks, xc, xh, fixed, fixed_s, bm, bt, mix, ex, cum, cumd, sdev, srecv, sq, got, tq, tback, give_b, tin,
    uhl, ehl, rows_sc, rex, ue, ee, yg, eg, cc, ab, sc0, sc1, pb0, pb1, mrow, lrow, ar0, ar1, acc,
    loc_s, a_s, a_r, halo_s, halo_r, z_s, z_r, row_s, row_r, sh_s, sh_r, st_s, st_r, tq_s, tq_r,
    sx_s, sx_r, tx_s, tx_r, out_s,
):
    s = lax.axis_index("seq")
    h = lax.axis_index("head")
    core = lax.rem(s, 2)
    x = lax.rem(s // 2, 4)
    z = s // 8
    first_row = s * T

    def at(zz, xx, cc_):
        return {"seq": (zz * 4 + xx) * 2 + cc_, "head": h}

    nz = lax.axis_size("seq") // 8
    z_next, z_prev = lax.rem(z + 1, nz), lax.rem(z + nz - 1, nz)
    right = [lax.rem(x + o, 4) for o in range(4)]
    left = [lax.rem(x + 4 - o, 4) for o in range(4)]
    sibling = at(z, x, 1 - core)
    above = at(z_next, x, core)
    after = {"seq": lax.rem(s + 1, nz * 8), "head": h}
    before = {"seq": lax.rem(s + nz * 8 - 1, nz * 8), "head": h}

    def peer(o):
        return lax.rem(h + o, 4)

    def remote(src, dst, ssem, rsem, target):
        return pltpu.make_async_remote_copy(
            src_ref=src, dst_ref=dst, send_sem=ssem, recv_sem=rsem, device_id=target, device_id_type=MESH
        )

    loads = [
        pltpu.make_async_copy(x_ref, xb.at[pl.ds(HALO, T)], loc_s.at[0]),
        pltpu.make_async_copy(bc_ref, bc3, loc_s.at[1]),
        pltpu.make_async_copy(step_ref, stt.at[pl.ds(0, NH)], loc_s.at[2]),
        pltpu.make_async_copy(gate_ref, gb, loc_s.at[3]),
        pltpu.make_async_copy(
            q_ref.at[:, pl.ds(pl.multiple_of(h * 512, 512), 512)],
            qb.at[pl.ds(pl.multiple_of(h * 96, 32), 96)], loc_s.at[4]),
        pltpu.make_async_copy(
            kv_ref.at[:, :, pl.ds(pl.multiple_of(h * 128, 128), 128)],
            kv3.at[pl.ds(pl.multiple_of(h * 96, 32), 96)], loc_s.at[5]),
    ]
    for copy in loads:
        copy.start()

    barrier = pltpu.get_barrier_semaphore()
    for o in (1, 2, 3):
        pl.semaphore_signal(barrier, inc=1, device_id={"seq": s, "head": peer(o)}, device_id_type=MESH)
    for target in (before, sibling):
        pl.semaphore_signal(barrier, inc=1, device_id=target, device_id_type=MESH)
    for o in (1, 2, 3):
        pl.semaphore_signal(barrier, inc=1, device_id=at(z, left[o], core), device_id_type=MESH)
    for o in (0, 1, 2, 3):
        pl.semaphore_signal(barrier, inc=1, device_id=at(z_prev, left[o], core), device_id_type=MESH)
    for o in (1, 2, 3):
        pl.semaphore_signal(
            barrier, inc=1, device_id={"seq": (z_prev * 4 + x) * 2 + core, "head": peer(o)}, device_id_type=MESH)

    def a2a(o, which):
        to = peer(o)
        target = {"seq": s, "head": to}
        mine = pl.ds(pl.multiple_of(h * 96, 32), 96)
        if which == 0:
            return remote(
                kv_ref.at[:, :, pl.ds(pl.multiple_of(to * 128, 128), 128)], kv3.at[mine],
                a_s.at[0, o - 1], a_r.at[0, o - 1], target)
        return remote(
            q_ref.at[:, pl.ds(pl.multiple_of(to * 512, 512), 512)], qb.at[mine],
            a_s.at[1, o - 1], a_r.at[1, o - 1], target)

    halo_x = remote(x_ref.at[pl.ds(T - HALO, HALO)], hx, halo_s.at[0], halo_r.at[0], after)
    halo_bc = remote(bc_ref.at[pl.ds(T - HALO, HALO)], hb3, halo_s.at[1], halo_r.at[1], after)
    exchange = [[a2a(o, w) for o in (1, 2, 3)] for w in (0, 1)]

    def block_half(d, i):
        return kvb.at[d, pl.ds(i * HT, HT), pl.ds(0, 256)]

    def rising(o):
        to = peer(o)
        return remote(
            kv_ref.at[:, :, pl.ds(pl.multiple_of(to * 128, 128), 128)], kv3z.at[pl.ds(pl.multiple_of(h * 96, 32), 96)],
            z_s.at[o], z_r.at[o], {"seq": (z_next * 4 + x) * 2 + core, "head": to})

    rise = [rising(o) for o in (0, 1, 2, 3)]

    def along(o, i, source):
        return remote(
            block_half(source, i), block_half(2 * o, i), row_s.at[o - 1, i], row_r.at[o - 1, i], at(z, right[o], core))

    def unpack(buffer, d):
        pair = jnp.swapaxes(buffer[...], 0, 1)
        kvb[d, :, pl.ds(0, 128)] = pair[1]
        kvb[d, :, pl.ds(128, 128)] = pair[0]

    def kv_own():
        loads[5].wait()
        for copy in exchange[0]:
            copy.wait_recv()
        unpack(kv3, 0)
        for i in (0, 1):
            for o in (1, 2, 3):
                pl.when(x + o < 4)(along(o, i, 0).start)
        share_slot(0)

    def kv_risen():
        for copy in rise:
            copy.wait_recv()
        unpack(kv3z, 8)
        for i in (0, 1):
            for o in (3, 2, 1):
                pl.when(x + o >= 4)(along(o, i, 8).start)
        share_slot(8)

    def kv_row(o):
        for i in (0, 1):
            along(o, i, 0).wait_recv()

    def share(i):
        return remote(
            kvb.at[2 * (i + core), :, pl.ds(0, 256)], kvb.at[2 * i + 1, :, pl.ds(0, 256)],
            sh_s.at[i], sh_r.at[i], sibling)

    def share_slot(d):
        if d == 0:
            pl.when(core == 0)(share(0).start)
        elif d == 8:
            pl.when(core == 1)(share(3).start)
        else:
            for c in (0, 1):
                pl.when(core == c)(share(d // 2 - c).start)

    def shared(d):
        if d in (0, 8):
            pl.when(core == 1)(share(0).wait_recv)
            pl.when(core == 0)(share(3).wait_recv)
        else:
            for c in (0, 1):
                pl.when(core == c)(share(d // 2 - 1 + c).wait_recv)

    ends, total = [], jnp.int32(0)
    for i in range(DOCS):
        total = total + dl_ref[i]
        ends.append(total)
    row = lax.broadcasted_iota(jnp.int32, (T, 128), 0)
    lane = lax.broadcasted_iota(jnp.int32, (T, 128), 1)
    pos = row + first_row
    begin = jnp.zeros((T, 128), jnp.int32)
    for i in range(DOCS):
        begin = jnp.where(ends[i] <= pos, ends[i], begin)
    start[...] = begin
    inside = pos - begin
    for lag in (1, 2, 3):
        masks[lag - 1] = jnp.where(inside >= lag, 1.0, 0.0)
    lane1 = lax.broadcasted_iota(jnp.int32, (1, 128), 1)
    doc_first = jnp.full((1, 128), 1 << 30, jnp.int32)
    doc_end = jnp.full((1, 128), 1 << 30, jnp.int32)
    for i in range(DOCS):
        doc_end = jnp.where(lane1 == i, ends[i], doc_end)
        doc_first = jnp.where(lane1 == i, ends[i - 1] if i else 0, doc_first)
    def expand_body(n, carry):
        r = lax.broadcasted_iota(jnp.int32, (128, 256), 0)
        c = lax.broadcasted_iota(jnp.int32, (128, 256), 1) + n * 256
        ex[:, pl.ds(pl.multiple_of(n * 256, 256), 256)] = jnp.where(
            (r < 2 * NH) & ((r & (NH - 1)) == (c >> 6)), 1.0, 0.0).astype(BF16)
        return carry

    lax.fori_loop(0, INNER // 256, expand_body, 0)

    rows_sc[...] = jnp.zeros_like(rows_sc)
    rows_sc[pl.ds(32, 1), pl.ds(0, NH)] = dec_ref[...].reshape(1, NH)
    rows_sc[pl.ds(25, 1), pl.ds(0, NH)] = skip_ref[...].reshape(1, NH)
    loads[2].wait()
    stt[pl.ds(NH, 128 - NH)] = jnp.zeros((128 - NH, T), F32)
    step = jnp.transpose(stt[...])
    a = -(step * rows_sc[pl.ds(32, 1), :])
    a1 = a.astype(BF16).astype(F32)
    a2 = (a - a1).astype(BF16).astype(F32)
    a3 = a - a1 - a2
    parts = (a1 + pltpu.roll(a2, 32, 1) + pltpu.roll(a3, 64, 1)).astype(BF16)
    tr = lax.broadcasted_iota(jnp.int32, (T, T), 0)
    tc = lax.broadcasted_iota(jnp.int32, (T, T), 1)
    tri = jnp.where(tc <= tr, 1.0, 0.0)
    tri_ch = jnp.where((tc <= tr) & ((tc >> 6) == (tr >> 6)), 1.0, 0.0)

    def collect(t):
        v = mm(t.astype(BF16), parts)
        v = v + pltpu.roll(v, 96, 1) + pltpu.roll(v, 64, 1)
        return jnp.where(lane < NH, v, 0.0)

    cum[...] = collect(tri_ch)
    cumd[...] = collect(tri)
    for c in range(NC):
        rc = pl.ds(c * CH, CH)
        cu = cum[rc, :]
        mid = cum[pl.ds(c * CH + CH // 2 - 1, 1), :]
        end = cum[pl.ds(c * CH + CH - 1, 1), :]
        uhl[rc, :] = split_rows(jnp.exp(cu - mid))
        through = jnp.where(start[pl.ds(c * CH + CH - 1, 1), :] < first_row + c * CH, 1.0, 0.0)
        rows_sc[pl.ds(c, 1), :] = jnp.exp(mid)
        rows_sc[pl.ds(8 + c, 1), :] = jnp.exp(end - mid)
        rows_sc[pl.ds(16 + c, 1), :] = jnp.exp(end) * through
        cum[rc, :] = step[c * CH : (c + 1) * CH] * jnp.exp(mid - cu)
    open_dev = jnp.where(start[pl.ds(T - 1, 1), :] < first_row, 1.0, 0.0)
    rows_sc[pl.ds(24, 1), :] = jnp.exp(cumd[pl.ds(T - 1, 1), :]) * open_dev
    ehl[...] = split_rows(jnp.where(start[...] < first_row, jnp.exp(cumd[...]), 0.0))
    rex[...] = mm(split_rows(rows_sc[pl.ds(0, 32), :]), ex[...])
    svhl = split_rows(cum[...])

    pl.semaphore_wait(barrier, 15)
    halo_x.start()
    halo_bc.start()
    for copy in exchange[0] + rise:
        copy.start()

    loads[0].wait()
    loads[1].wait()
    xb[pl.ds(0, HALO), :] = jnp.zeros((HALO, INNER), BF16)
    bcb[pl.ds(0, HALO), :] = jnp.zeros((HALO, 512), BF16)
    split = jnp.swapaxes(bc3[...], 0, 1)
    bcb[pl.ds(HALO, T), pl.ds(0, 256)] = split[0]
    bcb[pl.ds(HALO, T), pl.ds(256, 256)] = split[1]
    taps_bc = jnp.swapaxes(cbc_ref[...], 0, 1).astype(F32)
    cbc[:, pl.ds(0, 256)] = taps_bc[0]
    cbc[:, pl.ds(256, 256)] = taps_bc[1]

    def convolve(src, cols, weight, cf):
        cf[...] = src[:, cols].astype(F32)
        out = cf[pl.ds(HALO, T), :] * weight[3:4]
        for lag in (1, 2, 3):
            out = out + cf[pl.ds(HALO - lag, T), :] * masks[lag - 1] * weight[3 - lag : 4 - lag]
        return silu(out).astype(BF16)

    def conv_bc(n, carry):
        cols = pl.ds(pl.multiple_of(n * 128, 128), 128)
        out = convolve(bcb, cols, cbc[:, cols], cf0)

        @pl.when(n < 2)
        def _():
            bm[:, cols] = out

        @pl.when(n >= 2)
        def _():
            cc[:, pl.ds(pl.multiple_of(n * 128 - 256, 128), 128)] = out
        return carry

    lax.fori_loop(0, 4, conv_bc, 0)

    def conv_quarter(o):
        def body(g, carry):
            first = g * GC + right[o] * NQ
            both_cols = pl.ds(pl.multiple_of(first, NQ), NQ)
            out = []
            for k, cf in enumerate((cf0, cf1)):
                cols = pl.ds(pl.multiple_of(first + k * 128, 128), 128)
                out.append(convolve(xb, cols, cx_ref[:, cols].astype(F32), cf))
                xc[:, cols] = out[-1]
            scale = mm(svhl, ex[:, both_cols])
            for k in (0, 1):
                cols = pl.ds(pl.multiple_of(first + k * 128, 128), 128)
                scaled = (out[k].astype(F32) * scale[:, k * 128 : (k + 1) * 128]).astype(BF16)
                for c in range(NC):
                    xh[c, pl.ds(ST, CH), cols] = scaled[c * CH : (c + 1) * CH]
            return carry

        lax.fori_loop(0, 2, body, 0)

    order = (2, 1, 3, 0)

    conv_quarter(order[0])
    conv_quarter(order[1])

    conv_quarter(order[2])
    conv_quarter(order[3])

    halo_x.wait_recv()
    halo_bc.wait_recv()

    def first_rows(halo, own, weight):
        width = own.shape[1]
        v = jnp.concatenate([halo, own], 0).astype(F32)
        out = v[HALO:] * weight[3:4]
        for lag in (1, 2, 3):
            mask = jnp.concatenate([masks[lag - 1, pl.ds(0, HALO), :]] * (width // 128), 1)
            out = out + pltpu.roll(v, lag, 0)[HALO:] * mask * weight[3 - lag : 4 - lag]
        return silu(out).astype(BF16)

    halo_pair = jnp.swapaxes(hb3[...], 0, 1)
    head_rows, own_rows = pl.ds(0, HALO), pl.ds(HALO, HALO)
    bm[head_rows, :] = first_rows(halo_pair[0], bcb[own_rows, pl.ds(0, 256)], cbc[:, pl.ds(0, 256)])
    cc[head_rows, :] = first_rows(halo_pair[1], bcb[own_rows, pl.ds(256, 256)], cbc[:, pl.ds(256, 256)])
    for n in range(4):
        cols = pl.ds(n * 512, 512)
        out = first_rows(hx[:, cols], xb[own_rows, cols], cx_ref[:, cols].astype(F32))
        fixed[:, cols] = out
        fixed_s[:, cols] = (out.astype(F32) * mm(svhl[:HALO], ex[:, cols])).astype(BF16)

    out_c = pltpu.make_async_copy(cc, cc_ref, out_s.at[3])
    out_c.start()

    for c in range(NC):
        last = start[pl.ds(c * CH + CH - 1, 1), :]
        reach = pos[c * CH : (c + 1) * CH] >= last
        for g in (0, 1):
            b = jnp.where(reach, bm[pl.ds(c * CH, CH), pl.ds(g * 128, 128)].astype(F32), 0.0)
            bt[g, c] = jnp.transpose(b).astype(BF16)

    def end_states(o):
        quarter = right[o]

        def body(g, carry):
            cols = pl.ds(pl.multiple_of(g * GC + quarter * NQ, NQ), NQ)
            xc[head_rows, cols] = fixed[:, cols]
            xh[0, pl.ds(ST, HALO), cols] = fixed_s[:, cols]
            state = None
            for c in range(NC):
                if c == 0:
                    xh[c, pl.ds(0, ST), cols] = jnp.zeros((ST, NQ), BF16)
                else:
                    xh[c, pl.ds(0, ST), cols] = (state * rex[pl.ds(c, 1), cols]).astype(BF16)
                new = mm(bt[g, c], xh[c, pl.ds(ST, CH), cols])
                new = new * rex[pl.ds(8 + c, 1), cols]
                state = new if c == 0 else state * rex[pl.ds(16 + c, 1), cols] + new
            sdev[g, quarter, pl.ds(0, ST), :] = state.astype(BF16)
            d = jnp.broadcast_to(rex[pl.ds(24, 1), cols], (8, NQ))
            high = d.astype(BF16).astype(F32)
            sdev[g, quarter, pl.ds(ST, 16), :] = jnp.concatenate([high, d - high], 0).astype(BF16)
            return carry

        lax.fori_loop(0, 2, body, 0)

    def swap(o):
        return remote(
            sdev.at[1 - core, right[o]], srecv.at[right[o]], sx_s.at[o], sx_r.at[o], sibling)

    def decay_of(ref):
        d = ref[pl.ds(ST, 16), :].astype(F32)
        return d[0:1] + d[8:9]

    def both(quarter):
        mine, other = sdev.at[core, quarter], srecv.at[quarter]
        sm, so = mine[pl.ds(0, ST), :].astype(F32), other[pl.ds(0, ST), :].astype(F32)
        dm, do = decay_of(mine), decay_of(other)
        first = core == 0
        return (jnp.where(first, sm, so), jnp.where(first, dm, do), jnp.where(first, so, sm), jnp.where(first, do, dm))

    def deal_up(o):
        return remote(sq.at[right[o]], got.at[1, x], st_s.at[3 + o], st_r.at[3 + o], at(z_next, right[o], core))

    def deal_row(o):
        return remote(sq.at[right[o]], got.at[0, x], st_s.at[o - 1], st_r.at[o - 1], at(z, right[o], core))

    def chip_state(o):
        quarter = right[o]
        swap(o).wait_recv()
        s0, d0, s1, d1 = both(quarter)
        sq[quarter, pl.ds(0, ST), :] = (s0 * d1 + s1).astype(BF16)
        d = jnp.broadcast_to(d0 * d1, (8, NQ))
        high = d.astype(BF16).astype(F32)
        sq[quarter, pl.ds(ST, 16), :] = jnp.concatenate([high, d - high], 0).astype(BF16)
        deal_up(o).start()
        if o:
            pl.when(x < 3)(deal_row(o).start)

    kv_own()
    for copy in exchange[1]:
        copy.start()
    end_states(order[0])
    swap(order[0]).start()
    end_states(order[1])
    swap(order[1]).start()
    chip_state(order[0])
    end_states(order[2])
    swap(order[2]).start()
    chip_state(order[1])
    kv_risen()
    end_states(order[3])
    swap(order[3]).start()
    chip_state(order[2])
    chip_state(order[3])

    for d in range(9):
        block = lax.rem(s + BLOCKS - d, BLOCKS)
        key = row + block * T
        hot = (key >= doc_first) & (key < doc_end)
        kvb[d, :, pl.ds(256, 128)] = jnp.where(hot, 1.0, 0.0).astype(BF16)
        if d == 0:
            blind = jnp.where(hot | (lane >= DOCS), 0.0, MASKED).astype(BF16)
            for i in range(QH):
                qa[i, :, pl.ds(128, 128)] = blind

    loads[4].wait()
    for copy in exchange[1]:
        copy.wait_recv()
    for i in range(QH):
        qa[i, :, pl.ds(0, 128)] = qb[:, pl.ds(i * 128, 128)]

    got[0, x] = sq[x]

    RT = 128
    scs, pbs, ars = (sc0, sc1), (pb0, pb1), (ar0, ar1)

    def attend(slots, first):
        tiles = T * len(slots) // 128

        def scores(i):
            for n, d in enumerate(slots):
                scs[i % 2][:, pl.ds(n * T, T)] = mm_nt(qa[i], kvb[d, :, pl.ds(128, 256)])

        def block(i, r, k):
            v = scs[i % 2][pl.ds(r * RT, RT), pl.ds(k * 128, 128)]
            if first and k == r:
                rr = lax.broadcasted_iota(jnp.int32, (RT, 128), 0)
                cc_ = lax.broadcasted_iota(jnp.int32, (RT, 128), 1)
                v = jnp.where(cc_ <= rr, v, MASKED)
            return v

        def highest(i, r):
            rs = pl.ds(r * RT, RT)
            top = block(i, r, 0)
            for k in range(1, r + 1 if first else tiles):
                top = jnp.maximum(top, block(i, r, k))
            top = jnp.max(top, axis=1, keepdims=True)
            if first:
                mrow[i, rs, :] = jnp.broadcast_to(top, (RT, 128))
            else:
                old = mrow[i, rs, :]
                new = jnp.maximum(old, top)
                ars[i % 2][rs, :] = jnp.exp2((old - new) * SCORE)
                mrow[i, rs, :] = new

        def weigh(i, r):
            rs = pl.ds(r * RT, RT)
            new, part = mrow[i, rs, :], None
            for k in range(tiles):
                if first and k > r:
                    pbs[i % 2][rs, pl.ds(k * 128, 128)] = jnp.zeros((RT, 128), BF16)
                    continue
                p = jnp.exp2((block(i, r, k) - new) * SCORE)
                part = p if part is None else part + p
                pbs[i % 2][rs, pl.ds(k * 128, 128)] = p.astype(BF16)
            lrow[i, rs, :] = part if first else lrow[i, rs, :] * ars[i % 2][rs, :] + part

        def gather(i):
            out = mm(pbs[i % 2][:, pl.ds(0, T)], kvb[slots[0], :, pl.ds(0, 128)])
            for n, d in enumerate(slots[1:]):
                out = out + mm(pbs[i % 2][:, pl.ds((n + 1) * T, T)], kvb[d, :, pl.ds(0, 128)])
            acc[i] = out if first else acc[i] * ars[i % 2][...] + out

        scores(0)
        for i in range(QH):
            if i + 1 < QH:
                scores(i + 1)
            if i > 0:
                gather(i - 1)
            for r in range(T // RT):
                highest(i, r)
            for r in range(T // RT):
                weigh(i, r)
        gather(QH - 1)

    attend((0,), True)

    loads[3].wait()

    for c in range(NC):
        rc = pl.ds(c * CH, CH)
        begin = start[rc, :]
        base = first_row + c * CH
        tpos = lax.broadcasted_iota(jnp.int32, (CH, CH), 0)
        spos = lax.broadcasted_iota(jnp.int32, (CH, CH), 1)
        for g in (0, 1):
            gl = pl.ds(g * 128, 128)
            cg = cc[rc, gl]
            grid = mm_nt(cg, bm[rc, gl])
            grid = jnp.where((spos <= tpos) & (spos + base >= begin[:, :CH]), grid, 0.0).astype(BF16)
            mix[g, c, :, pl.ds(0, 128)] = jnp.where(begin < base, cg.astype(F32), 0.0).astype(BF16)
            mix[g, c, :, pl.ds(128, CH)] = grid

    def local(n, carry):
        g = n >> 2
        cols = pl.ds(pl.multiple_of(n * 256, 256), 256)
        ue[...] = mm(uhl[...], ex[:, cols])
        ee[...] = mm(ehl[...], ex[:, cols])
        for c in range(NC):
            rc = pl.ds(c * CH, CH)
            y = mm(mix[g, c], xh[c, :, cols])
            y = y * ue[rc, :] + rex[pl.ds(25, 1), cols] * xc[rc, cols].astype(F32)
            sg = silu(gb[rc, cols].astype(F32))
            yg[rc, cols] = (y * sg).astype(BF16)
            eg[rc, cols] = (ee[rc, :] * sg).astype(BF16)
        pltpu.make_async_copy(yg.at[:, cols], yg_ref.at[:, cols], out_s.at[1]).start()
        pltpu.make_async_copy(eg.at[:, cols], eg_ref.at[:, cols], out_s.at[2]).start()
        return carry

    def locals_(lo, hi):
        lax.fori_loop(lo, hi, local, 0)

    locals_(0, 4)
    shared(8)
    attend((8, 7 - 6 * core), False)

    for o in order:
        deal_up(o).wait_recv()
        if o:
            pl.when(left[o] < 3)(deal_row(o).wait_recv)

    def decay(r, j):
        d = got[r, j, pl.ds(ST, 16), :].astype(F32)
        return d[0:1] + d[8:9]

    def entering(n, carry):
        rs = pl.ds(pl.multiple_of(n * 32, 32), 32)
        later, fall = [None] * 4, None
        for j in (3, 2, 1, 0):
            v = got[1, j, rs, :].astype(F32)
            later[j] = v if j == 3 else later[j + 1] + fall * v
            fall = decay(1, j) if j == 3 else fall * decay(1, j)
        tq[0, rs, :] = later[0].astype(BF16)
        for j in (0, 1, 2):
            v = got[0, j, rs, :].astype(F32)
            row_sum = v if j == 0 else v + decay(0, j) * row_sum
            fall = decay(0, j) if j == 0 else fall * decay(0, j)
            tq[j + 1, rs, :] = (row_sum + fall * later[j + 1]).astype(BF16)
        return carry

    lax.fori_loop(0, ST // 32, entering, 0)
    back = [
        remote(tq.at[right[o]], tback.at[x], tq_s.at[o - 1], tq_r.at[o - 1], at(z, right[o], core)) for o in (1, 2, 3)
    ]
    for copy in back:
        copy.start()
    tback[x] = tq[x]

    locals_(4, 6)
    for o in (1, 2, 3):
        kv_row(o)
        share_slot(2 * o)
    locals_(6, 8)
    shared(2)
    shared(4)
    attend((2, 1 + 2 * core, 4, 3 + 2 * core), False)
    for copy in back:
        copy.wait_recv()

    def enter(n, carry):
        cols = pl.ds(pl.multiple_of(n * NQ, NQ), NQ)
        t = tback[n].astype(F32)
        s0, d0, _, _ = both(n)
        t1 = s0 + d0 * t
        first = core == 0
        tin[core, :, cols] = jnp.where(first, t, t1).astype(BF16)
        give_b[:, cols] = jnp.where(first, t1, t).astype(BF16)
        return carry

    lax.fori_loop(0, 4, enter, 0)
    give = remote(give_b, tin.at[core], tx_s, tx_r, sibling)
    give.start()
    shared(6)
    attend((6, 5 + 2 * core), False)

    def finish_head(i, carry):
        total = jnp.sum(lrow[i], axis=1, keepdims=True)
        ab[:, pl.ds(pl.multiple_of(i * 128, 128), 128)] = (acc[i] / total).astype(BF16)
        return carry

    lax.fori_loop(0, QH, finish_head, 0)
    out_a = pltpu.make_async_copy(ab, ao_ref, out_s.at[0])
    out_a.start()

    remote(give_b, tin.at[1 - core], tx_s, tx_r, sibling).wait_recv()

    out_t = pltpu.make_async_copy(tin, tin_ref, out_s.at[4])
    out_t.start()

    for group in exchange:
        for copy in group:
            copy.wait_send()
    halo_x.wait_send()
    halo_bc.wait_send()
    for copy in rise:
        copy.wait_send()
    for i in (0, 1):
        for o in (1, 2, 3):
            along(o, i, 0).wait_send()
    for o in order:
        swap(o).wait_send()
        deal_up(o).wait_send()
        if o:
            pl.when(x < 3)(deal_row(o).wait_send)
    for copy in back:
        copy.wait_send()
    for i in range(4):
        share(i).wait_send()
    give.wait_send()
    out_a.wait()
    pltpu.make_async_copy(yg, yg_ref, out_s.at[1]).wait()
    pltpu.make_async_copy(eg, eg_ref, out_s.at[2]).wait()
    out_c.wait()
    out_t.wait()

TR = 128
SUB = 16


def finish(yg_ref, eg_ref, cc_ref, tin_ref, gain_ref, a_ref, mo_ref, ao_ref, yg, eg, cc, tin, ab, far, ob, in_s, row_s, out_s):
    small = [pltpu.make_async_copy(tin_ref, tin, in_s.at[0]), pltpu.make_async_copy(cc_ref, cc, in_s.at[1])]
    large = []
    for i in range(T // TR):
        r = pl.ds(i * TR, TR)
        large.append((
            pltpu.make_async_copy(yg_ref.at[r], yg.at[r], row_s.at[0, i]),
            pltpu.make_async_copy(eg_ref.at[r], eg.at[r], row_s.at[1, i])))
    came = pltpu.make_async_copy(a_ref, ab, in_s.at[2])
    for copy in small + [copy for pair in large for copy in pair] + [came]:
        copy.start()
    for copy in small:
        copy.wait()
    attention = pltpu.make_async_copy(ab, ao_ref, out_s.at[T // TR])
    outs = [attention]
    for i in range(T // TR):
        r = pl.ds(i * TR, TR)
        for copy in large[i]:
            copy.wait()
        for g in range(2):
            cols = pl.ds(g * GC, GC)
            gain = gain_ref[cols].reshape(1, GC)
            far[r, cols] = mm(cc[r, pl.ds(g * 128, 128)], tin[g])
            for k in range(TR // SUB):
                q = pl.ds(i * TR + k * SUB, SUB)
                gated = yg[q, cols].astype(F32) + eg[q, cols].astype(F32) * far[q, cols]
                mean = jnp.sum(gated * gated, axis=1, keepdims=True) * (1.0 / GC)
                scale = lax.rsqrt(mean + EPSILON)
                ob[q, cols] = (gated * scale * gain).astype(BF16)
        outs.append(pltpu.make_async_copy(ob.at[r], mo_ref.at[r], out_s.at[i]))
        outs[-1].start()
    came.wait()
    attention.start()
    for copy in outs:
        copy.wait()


def per_device(
    x_in, bc_in, gate_in, step_size, decay_rate, skip, conv_x, conv_bc, norm_gain, queries, keys_values, doc_lengths
):
    vm, hbm = pl.BlockSpec(memory_space=pltpu.VMEM), pl.BlockSpec(memory_space=pltpu.HBM)
    dma = pltpu.SemaphoreType.DMA
    V = pltpu.VMEM
    shape = jax.ShapeDtypeStruct
    main = pl.pallas_call(
        kernel,
        out_shape=(
            shape((T, INNER), BF16), shape((T, INNER), BF16), shape((T, 256), BF16),
            shape((2, ST, GC), BF16), shape((T, QH * AD), BF16),
        ),
        in_specs=[pl.BlockSpec(memory_space=pltpu.SMEM)] + [vm] * 4 + [hbm] * 6,
        out_specs=(hbm,) * 5,
        scratch_shapes=[
            V((HALO + T, INNER), BF16),
            V((HALO, INNER), BF16),
            V((T, 2, 256), BF16),
            V((HALO, 2, 256), BF16),
            V((HALO + T, 512), BF16),
            V((4, 512), F32),
            V((T, INNER), BF16),
            V((128, T), F32),
            V((T, 512), BF16),
            V((QH, T, 256), BF16),
            V((T, 2, 128), BF16),
            V((T, 2, 128), BF16),
            V((9, T, 384), BF16),
            V((HALO + T, 128), F32),
            V((HALO + T, 128), F32),
            V((T, 128), jnp.int32),
            V((3, T, 128), F32),
            V((T, INNER), BF16),
            V((NC, ST + CH, INNER), BF16),
            V((HALO, INNER), BF16),
            V((HALO, INNER), BF16),
            V((T, 256), BF16),
            V((2, NC, ST, CH), BF16),
            V((2, NC, CH, ST + CH), BF16),
            V((128, INNER), BF16),
            V((T, 128), F32),
            V((T, 128), F32),
            V((2, 4, ST + 16, NQ), BF16),
            V((4, ST + 16, NQ), BF16),
            V((4, ST + 16, NQ), BF16),
            V((2, 4, ST + 16, NQ), BF16),
            V((4, ST, NQ), BF16),
            V((4, ST, NQ), BF16),
            V((ST, GC), BF16),
            V((2, ST, GC), BF16),
            V((T, 128), BF16),
            V((T, 128), BF16),
            V((40, 128), F32),
            V((32, INNER), F32),
            V((T, 256), F32),
            V((T, 256), F32),
            V((T, INNER), BF16),
            V((T, INNER), BF16),
            V((T, 256), BF16),
            V((T, 512), BF16),
            V((T, 4 * T), F32),
            V((T, 4 * T), F32),
            V((T, 4 * T), BF16),
            V((T, 4 * T), BF16),
            V((QH, T, 128), F32),
            V((QH, T, 128), F32),
            V((T, 128), F32),
            V((T, 128), F32),
            V((QH, T, 128), F32),
            dma((6,)),
            dma((2, 3)),
            dma((2, 3)),
            dma((2,)),
            dma((2,)),
            dma((4,)),
            dma((4,)),
            dma((3, 2)),
            dma((3, 2)),
            dma((4,)),
            dma((4,)),
            dma((7,)),
            dma((7,)),
            dma((3,)),
            dma((3,)),
            dma((4,)),
            dma((4,)),
            dma,
            dma,
            dma((5,)),
        ],
        compiler_params=pltpu.CompilerParams(
            collective_id=0, has_side_effects=True, vmem_limit_bytes=60 * 1024 * 1024
        ),
        name="hybrid",
    )
    yg, eg, cc, tin, attended = main(
        doc_lengths, decay_rate, skip, conv_x, conv_bc, x_in, bc_in, gate_in, step_size.T, queries, keys_values)
    return pl.pallas_call(
        finish,
        out_shape=(shape((T, INNER), BF16), shape((T, QH * AD), BF16)),
        in_specs=[hbm] * 4 + [vm, hbm],
        out_specs=(hbm, hbm),
        scratch_shapes=[
            V((T, INNER), BF16), V((T, INNER), BF16), V((T, 256), BF16), V((2, ST, GC), BF16), V((T, QH * AD), BF16),
            V((T, INNER), F32), V((T, INNER), BF16), dma((3,)), dma((2, T // TR)), dma((T // TR + 1,)),
        ],
        compiler_params=pltpu.CompilerParams(vmem_limit_bytes=60 * 1024 * 1024),
        name="finish",
    )(yg, eg, cc, tin, norm_gain, attended)


def solution(mesh):
    placed = (
        P("seq", "head"),
        P("seq", None, "head"),
        P("seq", "head"),
        P("seq", "head"),
        P("head"),
        P("head"),
        P(None, "head"),
        P(None, None, "head"),
        P("head"),
        P(("seq", "head"), None),
        P(("seq", "head"), None, None),
        P(),
    )
    return jax.shard_map(
        per_device,
        mesh=mesh,
        in_specs=placed,
        out_specs=(P("seq", "head"), P("seq", "head")),
        check_vma=False,
    )
```

```python
import functools
import jax
import jax.numpy as jnp
from jax import lax
from jax.experimental import pallas as pl
from jax.experimental.pallas import tpu as pltpu
from jax.sharding import PartitionSpec as P

T = 384
CH = 64
NC = T // CH
HD = 64
ST = 128
NH = 32
GC = 1024
INNER = 2 * GC
AD = 128
QH = 4
DOCS = 16
HALO = 16
BLOCKS = 64
EPSILON = 1e-05
MASKED = -1e30
SCORE = 1.4426950408889634 / AD**0.5
MESH = pl.DeviceIdType.MESH
F32 = jnp.float32
BF16 = jnp.bfloat16
HT = T // 2
NQ = GC // 4


def mm(a, b):
    return jnp.dot(a, b, preferred_element_type=F32)


def mm_nt(a, b):
    return lax.dot_general(a, b, (((1,), (1,)), ((), ())), preferred_element_type=F32)


def silu(v):
    half = 0.5 * v
    return half + half * jnp.tanh(half)


def split_rows(v):
    lane = lax.broadcasted_iota(jnp.int32, v.shape, 1)
    v = jnp.where(lane < NH, v, 0.0)
    high = v.astype(BF16).astype(F32)
    return (high + pltpu.roll(v - high, NH, 1)).astype(BF16)


def kernel(
    dl_ref, dec_ref, skip_ref, cx_ref, cbc_ref,
    x_ref, bc_ref, gate_ref, step_ref, q_ref, kv_ref,
    yg_ref, eg_ref, cc_ref, tin_ref, ao_ref,
    xb, hx, bc3, hb3, bcb, cbc, gb, stt, qb, qa, kv3, kv3z, kvb, cf0, cf1, start, masks, xc, xh, fixed, fixed_s, bm, bt, mix, ex, cum, cumd, sdev, srecv, sq, got, tq, tback, give_b, tin,
    uhl, ehl, rows_sc, rex, ue, ee, yg, eg, cc, ab, sc0, sc1, pb0, pb1, mrow, lrow, ar0, ar1, acc,
    loc_s, a_s, a_r, halo_s, halo_r, z_s, z_r, row_s, row_r, sh_s, sh_r, st_s, st_r, tq_s, tq_r,
    sx_s, sx_r, tx_s, tx_r, out_s,
):
    s = lax.axis_index("seq")
    h = lax.axis_index("head")
    core = lax.rem(s, 2)
    x = lax.rem(s // 2, 4)
    z = s // 8
    first_row = s * T

    def at(zz, xx, cc_):
        return {"seq": (zz * 4 + xx) * 2 + cc_, "head": h}

    nz = lax.axis_size("seq") // 8
    z_next, z_prev = lax.rem(z + 1, nz), lax.rem(z + nz - 1, nz)
    right = [lax.rem(x + o, 4) for o in range(4)]
    left = [lax.rem(x + 4 - o, 4) for o in range(4)]
    sibling = at(z, x, 1 - core)
    above = at(z_next, x, core)
    after = {"seq": lax.rem(s + 1, nz * 8), "head": h}
    before = {"seq": lax.rem(s + nz * 8 - 1, nz * 8), "head": h}

    def peer(o):
        return lax.rem(h + o, 4)

    def remote(src, dst, ssem, rsem, target):
        return pltpu.make_async_remote_copy(
            src_ref=src, dst_ref=dst, send_sem=ssem, recv_sem=rsem, device_id=target, device_id_type=MESH
        )

    loads = [
        pltpu.make_async_copy(x_ref, xb.at[pl.ds(HALO, T)], loc_s.at[0]),
        pltpu.make_async_copy(bc_ref, bc3, loc_s.at[1]),
        pltpu.make_async_copy(step_ref, stt.at[pl.ds(0, NH)], loc_s.at[2]),
        pltpu.make_async_copy(gate_ref, gb, loc_s.at[3]),
        pltpu.make_async_copy(
            q_ref.at[:, pl.ds(pl.multiple_of(h * 512, 512), 512)],
            qb.at[pl.ds(pl.multiple_of(h * 96, 32), 96)], loc_s.at[4]),
        pltpu.make_async_copy(
            kv_ref.at[:, :, pl.ds(pl.multiple_of(h * 128, 128), 128)],
            kv3.at[pl.ds(pl.multiple_of(h * 96, 32), 96)], loc_s.at[5]),
    ]
    for copy in loads:
        copy.start()

    barrier = pltpu.get_barrier_semaphore()
    for o in (1, 2, 3):
        pl.semaphore_signal(barrier, inc=1, device_id={"seq": s, "head": peer(o)}, device_id_type=MESH)
    for target in (before, sibling):
        pl.semaphore_signal(barrier, inc=1, device_id=target, device_id_type=MESH)
    for o in (1, 2, 3):
        pl.semaphore_signal(barrier, inc=1, device_id=at(z, left[o], core), device_id_type=MESH)
    for o in (0, 1, 2, 3):
        pl.semaphore_signal(barrier, inc=1, device_id=at(z_prev, left[o], core), device_id_type=MESH)
    for o in (1, 2, 3):
        pl.semaphore_signal(
            barrier, inc=1, device_id={"seq": (z_prev * 4 + x) * 2 + core, "head": peer(o)}, device_id_type=MESH)

    def a2a(o, which):
        to = peer(o)
        target = {"seq": s, "head": to}
        mine = pl.ds(pl.multiple_of(h * 96, 32), 96)
        if which == 0:
            return remote(
                kv_ref.at[:, :, pl.ds(pl.multiple_of(to * 128, 128), 128)], kv3.at[mine],
                a_s.at[0, o - 1], a_r.at[0, o - 1], target)
        return remote(
            q_ref.at[:, pl.ds(pl.multiple_of(to * 512, 512), 512)], qb.at[mine],
            a_s.at[1, o - 1], a_r.at[1, o - 1], target)

    halo_x = remote(x_ref.at[pl.ds(T - HALO, HALO)], hx, halo_s.at[0], halo_r.at[0], after)
    halo_bc = remote(bc_ref.at[pl.ds(T - HALO, HALO)], hb3, halo_s.at[1], halo_r.at[1], after)
    exchange = [[a2a(o, w) for o in (1, 2, 3)] for w in (0, 1)]

    def block_half(d, i):
        return kvb.at[d, pl.ds(i * HT, HT), pl.ds(0, 256)]

    def rising(o):
        to = peer(o)
        return remote(
            kv_ref.at[:, :, pl.ds(pl.multiple_of(to * 128, 128), 128)], kv3z.at[pl.ds(pl.multiple_of(h * 96, 32), 96)],
            z_s.at[o], z_r.at[o], {"seq": (z_next * 4 + x) * 2 + core, "head": to})

    rise = [rising(o) for o in (0, 1, 2, 3)]

    def along(o, i, source):
        return remote(
            block_half(source, i), block_half(2 * o, i), row_s.at[o - 1, i], row_r.at[o - 1, i], at(z, right[o], core))

    def unpack(buffer, d):
        pair = jnp.swapaxes(buffer[...], 0, 1)
        kvb[d, :, pl.ds(0, 128)] = pair[1]
        kvb[d, :, pl.ds(128, 128)] = pair[0]

    def kv_own():
        loads[5].wait()
        for copy in exchange[0]:
            copy.wait_recv()
        unpack(kv3, 0)
        for i in (0, 1):
            for o in (1, 2, 3):
                pl.when(x + o < 4)(along(o, i, 0).start)
        share_slot(0)

    def kv_risen():
        for copy in rise:
            copy.wait_recv()
        unpack(kv3z, 8)
        for i in (0, 1):
            for o in (3, 2, 1):
                pl.when(x + o >= 4)(along(o, i, 8).start)
        share_slot(8)

    def kv_row(o):
        for i in (0, 1):
            along(o, i, 0).wait_recv()

    def share(i):
        return remote(
            kvb.at[2 * (i + core), :, pl.ds(0, 256)], kvb.at[2 * i + 1, :, pl.ds(0, 256)],
            sh_s.at[i], sh_r.at[i], sibling)

    def share_slot(d):
        if d == 0:
            pl.when(core == 0)(share(0).start)
        elif d == 8:
            pl.when(core == 1)(share(3).start)
        else:
            for c in (0, 1):
                pl.when(core == c)(share(d // 2 - c).start)

    def shared(d):
        if d in (0, 8):
            pl.when(core == 1)(share(0).wait_recv)
            pl.when(core == 0)(share(3).wait_recv)
        else:
            for c in (0, 1):
                pl.when(core == c)(share(d // 2 - 1 + c).wait_recv)

    ends, total = [], jnp.int32(0)
    for i in range(DOCS):
        total = total + dl_ref[i]
        ends.append(total)
    row = lax.broadcasted_iota(jnp.int32, (T, 128), 0)
    lane = lax.broadcasted_iota(jnp.int32, (T, 128), 1)
    pos = row + first_row
    begin = jnp.zeros((T, 128), jnp.int32)
    for i in range(DOCS):
        begin = jnp.where(ends[i] <= pos, ends[i], begin)
    start[...] = begin
    inside = pos - begin
    for lag in (1, 2, 3):
        masks[lag - 1] = jnp.where(inside >= lag, 1.0, 0.0)
    lane1 = lax.broadcasted_iota(jnp.int32, (1, 128), 1)
    doc_first = jnp.full((1, 128), 1 << 30, jnp.int32)
    doc_end = jnp.full((1, 128), 1 << 30, jnp.int32)
    for i in range(DOCS):
        doc_end = jnp.where(lane1 == i, ends[i], doc_end)
        doc_first = jnp.where(lane1 == i, ends[i - 1] if i else 0, doc_first)
    def expand_body(n, carry):
        r = lax.broadcasted_iota(jnp.int32, (128, 256), 0)
        c = lax.broadcasted_iota(jnp.int32, (128, 256), 1) + n * 256
        ex[:, pl.ds(pl.multiple_of(n * 256, 256), 256)] = jnp.where(
            (r < 2 * NH) & ((r & (NH - 1)) == (c >> 6)), 1.0, 0.0).astype(BF16)
        return carry

    lax.fori_loop(0, INNER // 256, expand_body, 0)

    rows_sc[...] = jnp.zeros_like(rows_sc)
    rows_sc[pl.ds(32, 1), pl.ds(0, NH)] = dec_ref[...].reshape(1, NH)
    rows_sc[pl.ds(25, 1), pl.ds(0, NH)] = skip_ref[...].reshape(1, NH)
    loads[2].wait()
    stt[pl.ds(NH, 128 - NH)] = jnp.zeros((128 - NH, T), F32)
    step = jnp.transpose(stt[...])
    a = -(step * rows_sc[pl.ds(32, 1), :])
    a1 = a.astype(BF16).astype(F32)
    a2 = (a - a1).astype(BF16).astype(F32)
    a3 = a - a1 - a2
    parts = (a1 + pltpu.roll(a2, 32, 1) + pltpu.roll(a3, 64, 1)).astype(BF16)
    tr = lax.broadcasted_iota(jnp.int32, (T, T), 0)
    tc = lax.broadcasted_iota(jnp.int32, (T, T), 1)
    tri = jnp.where(tc <= tr, 1.0, 0.0)
    tri_ch = jnp.where((tc <= tr) & ((tc >> 6) == (tr >> 6)), 1.0, 0.0)

    def collect(t):
        v = mm(t.astype(BF16), parts)
        v = v + pltpu.roll(v, 96, 1) + pltpu.roll(v, 64, 1)
        return jnp.where(lane < NH, v, 0.0)

    cum[...] = collect(tri_ch)
    cumd[...] = collect(tri)
    for c in range(NC):
        rc = pl.ds(c * CH, CH)
        cu = cum[rc, :]
        mid = cum[pl.ds(c * CH + CH // 2 - 1, 1), :]
        end = cum[pl.ds(c * CH + CH - 1, 1), :]
        uhl[rc, :] = split_rows(jnp.exp(cu - mid))
        through = jnp.where(start[pl.ds(c * CH + CH - 1, 1), :] < first_row + c * CH, 1.0, 0.0)
        rows_sc[pl.ds(c, 1), :] = jnp.exp(mid)
        rows_sc[pl.ds(8 + c, 1), :] = jnp.exp(end - mid)
        rows_sc[pl.ds(16 + c, 1), :] = jnp.exp(end) * through
        cum[rc, :] = step[c * CH : (c + 1) * CH] * jnp.exp(mid - cu)
    open_dev = jnp.where(start[pl.ds(T - 1, 1), :] < first_row, 1.0, 0.0)
    rows_sc[pl.ds(24, 1), :] = jnp.exp(cumd[pl.ds(T - 1, 1), :]) * open_dev
    ehl[...] = split_rows(jnp.where(start[...] < first_row, jnp.exp(cumd[...]), 0.0))
    rex[...] = mm(split_rows(rows_sc[pl.ds(0, 32), :]), ex[...])
    svhl = split_rows(cum[...])

    pl.semaphore_wait(barrier, 15)
    halo_x.start()
    halo_bc.start()
    for copy in exchange[0] + rise:
        copy.start()

    loads[0].wait()
    loads[1].wait()
    xb[pl.ds(0, HALO), :] = jnp.zeros((HALO, INNER), BF16)
    bcb[pl.ds(0, HALO), :] = jnp.zeros((HALO, 512), BF16)
    split = jnp.swapaxes(bc3[...], 0, 1)
    bcb[pl.ds(HALO, T), pl.ds(0, 256)] = split[0]
    bcb[pl.ds(HALO, T), pl.ds(256, 256)] = split[1]
    taps_bc = jnp.swapaxes(cbc_ref[...], 0, 1).astype(F32)
    cbc[:, pl.ds(0, 256)] = taps_bc[0]
    cbc[:, pl.ds(256, 256)] = taps_bc[1]

    def convolve(src, cols, weight, cf):
        cf[...] = src[:, cols].astype(F32)
        out = cf[pl.ds(HALO, T), :] * weight[3:4]
        for lag in (1, 2, 3):
            out = out + cf[pl.ds(HALO - lag, T), :] * masks[lag - 1] * weight[3 - lag : 4 - lag]
        return silu(out).astype(BF16)

    def conv_bc(n, carry):
        cols = pl.ds(pl.multiple_of(n * 128, 128), 128)
        out = convolve(bcb, cols, cbc[:, cols], cf0)

        @pl.when(n < 2)
        def _():
            bm[:, cols] = out

        @pl.when(n >= 2)
        def _():
            cc[:, pl.ds(pl.multiple_of(n * 128 - 256, 128), 128)] = out
        return carry

    lax.fori_loop(0, 4, conv_bc, 0)

    def conv_quarter(o):
        def body(g, carry):
            first = g * GC + right[o] * NQ
            both_cols = pl.ds(pl.multiple_of(first, NQ), NQ)
            out = []
            for k, cf in enumerate((cf0, cf1)):
                cols = pl.ds(pl.multiple_of(first + k * 128, 128), 128)
                out.append(convolve(xb, cols, cx_ref[:, cols].astype(F32), cf))
                xc[:, cols] = out[-1]
            scale = mm(svhl, ex[:, both_cols])
            for k in (0, 1):
                cols = pl.ds(pl.multiple_of(first + k * 128, 128), 128)
                scaled = (out[k].astype(F32) * scale[:, k * 128 : (k + 1) * 128]).astype(BF16)
                for c in range(NC):
                    xh[c, pl.ds(ST, CH), cols] = scaled[c * CH : (c + 1) * CH]
            return carry

        lax.fori_loop(0, 2, body, 0)

    order = (2, 1, 3, 0)

    conv_quarter(order[0])
    conv_quarter(order[1])

    conv_quarter(order[2])
    conv_quarter(order[3])

    halo_x.wait_recv()
    halo_bc.wait_recv()

    def first_rows(halo, own, weight):
        width = own.shape[1]
        v = jnp.concatenate([halo, own], 0).astype(F32)
        out = v[HALO:] * weight[3:4]
        for lag in (1, 2, 3):
            mask = jnp.concatenate([masks[lag - 1, pl.ds(0, HALO), :]] * (width // 128), 1)
            out = out + pltpu.roll(v, lag, 0)[HALO:] * mask * weight[3 - lag : 4 - lag]
        return silu(out).astype(BF16)

    halo_pair = jnp.swapaxes(hb3[...], 0, 1)
    head_rows, own_rows = pl.ds(0, HALO), pl.ds(HALO, HALO)
    bm[head_rows, :] = first_rows(halo_pair[0], bcb[own_rows, pl.ds(0, 256)], cbc[:, pl.ds(0, 256)])
    cc[head_rows, :] = first_rows(halo_pair[1], bcb[own_rows, pl.ds(256, 256)], cbc[:, pl.ds(256, 256)])
    for n in range(4):
        cols = pl.ds(n * 512, 512)
        out = first_rows(hx[:, cols], xb[own_rows, cols], cx_ref[:, cols].astype(F32))
        fixed[:, cols] = out
        fixed_s[:, cols] = (out.astype(F32) * mm(svhl[:HALO], ex[:, cols])).astype(BF16)

    out_c = pltpu.make_async_copy(cc, cc_ref, out_s.at[3])
    out_c.start()

    for c in range(NC):
        last = start[pl.ds(c * CH + CH - 1, 1), :]
        reach = pos[c * CH : (c + 1) * CH] >= last
        for g in (0, 1):
            b = jnp.where(reach, bm[pl.ds(c * CH, CH), pl.ds(g * 128, 128)].astype(F32), 0.0)
            bt[g, c] = jnp.transpose(b).astype(BF16)

    def end_states(o):
        quarter = right[o]

        def body(g, carry):
            cols = pl.ds(pl.multiple_of(g * GC + quarter * NQ, NQ), NQ)
            xc[head_rows, cols] = fixed[:, cols]
            xh[0, pl.ds(ST, HALO), cols] = fixed_s[:, cols]
            state = None
            for c in range(NC):
                if c == 0:
                    xh[c, pl.ds(0, ST), cols] = jnp.zeros((ST, NQ), BF16)
                else:
                    xh[c, pl.ds(0, ST), cols] = (state * rex[pl.ds(c, 1), cols]).astype(BF16)
                new = mm(bt[g, c], xh[c, pl.ds(ST, CH), cols])
                new = new * rex[pl.ds(8 + c, 1), cols]
                state = new if c == 0 else state * rex[pl.ds(16 + c, 1), cols] + new
            sdev[g, quarter, pl.ds(0, ST), :] = state.astype(BF16)
            d = jnp.broadcast_to(rex[pl.ds(24, 1), cols], (8, NQ))
            high = d.astype(BF16).astype(F32)
            sdev[g, quarter, pl.ds(ST, 16), :] = jnp.concatenate([high, d - high], 0).astype(BF16)
            return carry

        lax.fori_loop(0, 2, body, 0)

    def swap(o):
        return remote(
            sdev.at[1 - core, right[o]], srecv.at[right[o]], sx_s.at[o], sx_r.at[o], sibling)

    def decay_of(ref):
        d = ref[pl.ds(ST, 16), :].astype(F32)
        return d[0:1] + d[8:9]

    def both(quarter):
        mine, other = sdev.at[core, quarter], srecv.at[quarter]
        sm, so = mine[pl.ds(0, ST), :].astype(F32), other[pl.ds(0, ST), :].astype(F32)
        dm, do = decay_of(mine), decay_of(other)
        first = core == 0
        return (jnp.where(first, sm, so), jnp.where(first, dm, do), jnp.where(first, so, sm), jnp.where(first, do, dm))

    def deal_up(o):
        return remote(sq.at[right[o]], got.at[1, x], st_s.at[3 + o], st_r.at[3 + o], at(z_next, right[o], core))

    def deal_row(o):
        return remote(sq.at[right[o]], got.at[0, x], st_s.at[o - 1], st_r.at[o - 1], at(z, right[o], core))

    def chip_state(o):
        quarter = right[o]
        swap(o).wait_recv()
        s0, d0, s1, d1 = both(quarter)
        sq[quarter, pl.ds(0, ST), :] = (s0 * d1 + s1).astype(BF16)
        d = jnp.broadcast_to(d0 * d1, (8, NQ))
        high = d.astype(BF16).astype(F32)
        sq[quarter, pl.ds(ST, 16), :] = jnp.concatenate([high, d - high], 0).astype(BF16)
        deal_up(o).start()
        if o:
            pl.when(x < 3)(deal_row(o).start)

    kv_own()
    for copy in exchange[1]:
        copy.start()
    end_states(order[0])
    swap(order[0]).start()
    end_states(order[1])
    swap(order[1]).start()
    chip_state(order[0])
    end_states(order[2])
    swap(order[2]).start()
    chip_state(order[1])
    kv_risen()
    end_states(order[3])
    swap(order[3]).start()
    chip_state(order[2])
    chip_state(order[3])

    for d in range(9):
        block = lax.rem(s + BLOCKS - d, BLOCKS)
        key = row + block * T
        hot = (key >= doc_first) & (key < doc_end)
        kvb[d, :, pl.ds(256, 128)] = jnp.where(hot, 1.0, 0.0).astype(BF16)
        if d == 0:
            blind = jnp.where(hot | (lane >= DOCS), 0.0, MASKED).astype(BF16)
            for i in range(QH):
                qa[i, :, pl.ds(128, 128)] = blind

    loads[4].wait()
    for copy in exchange[1]:
        copy.wait_recv()
    for i in range(QH):
        qa[i, :, pl.ds(0, 128)] = qb[:, pl.ds(i * 128, 128)]

    got[0, x] = sq[x]

    RT = 128
    scs, pbs, ars = (sc0, sc1), (pb0, pb1), (ar0, ar1)

    def attend(slots, first):
        tiles = T * len(slots) // 128

        def scores(i):
            for n, d in enumerate(slots):
                scs[i % 2][:, pl.ds(n * T, T)] = mm_nt(qa[i], kvb[d, :, pl.ds(128, 256)])

        def block(i, r, k):
            v = scs[i % 2][pl.ds(r * RT, RT), pl.ds(k * 128, 128)]
            if first and k == r:
                rr = lax.broadcasted_iota(jnp.int32, (RT, 128), 0)
                cc_ = lax.broadcasted_iota(jnp.int32, (RT, 128), 1)
                v = jnp.where(cc_ <= rr, v, MASKED)
            return v

        def highest(i, r):
            rs = pl.ds(r * RT, RT)
            top = block(i, r, 0)
            for k in range(1, r + 1 if first else tiles):
                top = jnp.maximum(top, block(i, r, k))
            top = jnp.max(top, axis=1, keepdims=True)
            if first:
                mrow[i, rs, :] = jnp.broadcast_to(top, (RT, 128))
            else:
                old = mrow[i, rs, :]
                new = jnp.maximum(old, top)
                ars[i % 2][rs, :] = jnp.exp2((old - new) * SCORE)
                mrow[i, rs, :] = new

        def weigh(i, r):
            rs = pl.ds(r * RT, RT)
            new, part = mrow[i, rs, :], None
            for k in range(tiles):
                if first and k > r:
                    pbs[i % 2][rs, pl.ds(k * 128, 128)] = jnp.zeros((RT, 128), BF16)
                    continue
                p = jnp.exp2((block(i, r, k) - new) * SCORE)
                part = p if part is None else part + p
                pbs[i % 2][rs, pl.ds(k * 128, 128)] = p.astype(BF16)
            lrow[i, rs, :] = part if first else lrow[i, rs, :] * ars[i % 2][rs, :] + part

        def gather(i):
            out = mm(pbs[i % 2][:, pl.ds(0, T)], kvb[slots[0], :, pl.ds(0, 128)])
            for n, d in enumerate(slots[1:]):
                out = out + mm(pbs[i % 2][:, pl.ds((n + 1) * T, T)], kvb[d, :, pl.ds(0, 128)])
            acc[i] = out if first else acc[i] * ars[i % 2][...] + out

        scores(0)
        for i in range(QH):
            if i + 1 < QH:
                scores(i + 1)
            if i > 0:
                gather(i - 1)
            for r in range(T // RT):
                highest(i, r)
            for r in range(T // RT):
                weigh(i, r)
        gather(QH - 1)

    attend((0,), True)

    loads[3].wait()

    for c in range(NC):
        rc = pl.ds(c * CH, CH)
        begin = start[rc, :]
        base = first_row + c * CH
        tpos = lax.broadcasted_iota(jnp.int32, (CH, CH), 0)
        spos = lax.broadcasted_iota(jnp.int32, (CH, CH), 1)
        for g in (0, 1):
            gl = pl.ds(g * 128, 128)
            cg = cc[rc, gl]
            grid = mm_nt(cg, bm[rc, gl])
            grid = jnp.where((spos <= tpos) & (spos + base >= begin[:, :CH]), grid, 0.0).astype(BF16)
            mix[g, c, :, pl.ds(0, 128)] = jnp.where(begin < base, cg.astype(F32), 0.0).astype(BF16)
            mix[g, c, :, pl.ds(128, CH)] = grid

    def local(n, carry):
        g = n >> 2
        cols = pl.ds(pl.multiple_of(n * 256, 256), 256)
        ue[...] = mm(uhl[...], ex[:, cols])
        ee[...] = mm(ehl[...], ex[:, cols])
        for c in range(NC):
            rc = pl.ds(c * CH, CH)
            y = mm(mix[g, c], xh[c, :, cols])
            y = y * ue[rc, :] + rex[pl.ds(25, 1), cols] * xc[rc, cols].astype(F32)
            sg = silu(gb[rc, cols].astype(F32))
            yg[rc, cols] = (y * sg).astype(BF16)
            eg[rc, cols] = (ee[rc, :] * sg).astype(BF16)
        pltpu.make_async_copy(yg.at[:, cols], yg_ref.at[:, cols], out_s.at[1]).start()
        pltpu.make_async_copy(eg.at[:, cols], eg_ref.at[:, cols], out_s.at[2]).start()
        return carry

    def locals_(lo, hi):
        lax.fori_loop(lo, hi, local, 0)

    locals_(0, 4)
    for o in order:
        deal_up(o).wait_recv()
        if o:
            pl.when(left[o] < 3)(deal_row(o).wait_recv)

    def decay(r, j):
        d = got[r, j, pl.ds(ST, 16), :].astype(F32)
        return d[0:1] + d[8:9]

    def entering(n, carry):
        rs = pl.ds(pl.multiple_of(n * 32, 32), 32)
        later, fall = [None] * 4, None
        for j in (3, 2, 1, 0):
            v = got[1, j, rs, :].astype(F32)
            later[j] = v if j == 3 else later[j + 1] + fall * v
            fall = decay(1, j) if j == 3 else fall * decay(1, j)
        tq[0, rs, :] = later[0].astype(BF16)
        for j in (0, 1, 2):
            v = got[0, j, rs, :].astype(F32)
            row_sum = v if j == 0 else v + decay(0, j) * row_sum
            fall = decay(0, j) if j == 0 else fall * decay(0, j)
            tq[j + 1, rs, :] = (row_sum + fall * later[j + 1]).astype(BF16)
        return carry

    lax.fori_loop(0, ST // 32, entering, 0)
    back = [
        remote(tq.at[right[o]], tback.at[x], tq_s.at[o - 1], tq_r.at[o - 1], at(z, right[o], core)) for o in (1, 2, 3)
    ]
    for copy in back:
        copy.start()
    tback[x] = tq[x]

    shared(8)
    attend((8, 7 - 6 * core), False)

    locals_(4, 6)
    for o in (1, 2, 3):
        kv_row(o)
        share_slot(2 * o)
    locals_(6, 8)
    shared(2)
    shared(4)
    attend((2, 1 + 2 * core, 4, 3 + 2 * core), False)
    for copy in back:
        copy.wait_recv()

    def enter(n, carry):
        cols = pl.ds(pl.multiple_of(n * NQ, NQ), NQ)
        t = tback[n].astype(F32)
        s0, d0, _, _ = both(n)
        t1 = s0 + d0 * t
        first = core == 0
        tin[core, :, cols] = jnp.where(first, t, t1).astype(BF16)
        give_b[:, cols] = jnp.where(first, t1, t).astype(BF16)
        return carry

    lax.fori_loop(0, 4, enter, 0)
    give = remote(give_b, tin.at[core], tx_s, tx_r, sibling)
    give.start()
    shared(6)
    attend((6, 5 + 2 * core), False)

    def finish_head(i, carry):
        total = jnp.sum(lrow[i], axis=1, keepdims=True)
        ab[:, pl.ds(pl.multiple_of(i * 128, 128), 128)] = (acc[i] / total).astype(BF16)
        return carry

    lax.fori_loop(0, QH, finish_head, 0)
    out_a = pltpu.make_async_copy(ab, ao_ref, out_s.at[0])
    out_a.start()

    remote(give_b, tin.at[1 - core], tx_s, tx_r, sibling).wait_recv()

    out_t = pltpu.make_async_copy(tin, tin_ref, out_s.at[4])
    out_t.start()

    for group in exchange:
        for copy in group:
            copy.wait_send()
    halo_x.wait_send()
    halo_bc.wait_send()
    for copy in rise:
        copy.wait_send()
    for i in (0, 1):
        for o in (1, 2, 3):
            along(o, i, 0).wait_send()
    for o in order:
        swap(o).wait_send()
        deal_up(o).wait_send()
        if o:
            pl.when(x < 3)(deal_row(o).wait_send)
    for copy in back:
        copy.wait_send()
    for i in range(4):
        share(i).wait_send()
    give.wait_send()
    out_a.wait()
    pltpu.make_async_copy(yg, yg_ref, out_s.at[1]).wait()
    pltpu.make_async_copy(eg, eg_ref, out_s.at[2]).wait()
    out_c.wait()
    out_t.wait()

TR = 128
SUB = 16


def finish(yg_ref, eg_ref, cc_ref, tin_ref, gain_ref, a_ref, mo_ref, ao_ref, yg, eg, cc, tin, ab, far, ob, in_s, row_s, out_s):
    small = [pltpu.make_async_copy(tin_ref, tin, in_s.at[0]), pltpu.make_async_copy(cc_ref, cc, in_s.at[1])]
    large = []
    for i in range(T // TR):
        r = pl.ds(i * TR, TR)
        large.append((
            pltpu.make_async_copy(yg_ref.at[r], yg.at[r], row_s.at[0, i]),
            pltpu.make_async_copy(eg_ref.at[r], eg.at[r], row_s.at[1, i])))
    came = pltpu.make_async_copy(a_ref, ab, in_s.at[2])
    for copy in small + [copy for pair in large for copy in pair] + [came]:
        copy.start()
    for copy in small:
        copy.wait()
    attention = pltpu.make_async_copy(ab, ao_ref, out_s.at[2 * (T // TR)])
    outs = [attention]
    for i in range(T // TR):
        r = pl.ds(i * TR, TR)
        for copy in large[i]:
            copy.wait()
        for g in range(2):
            cols = pl.ds(g * GC, GC)
            gain = gain_ref[cols].reshape(1, GC)
            far[r, cols] = mm(cc[r, pl.ds(g * 128, 128)], tin[g])
            for k in range(TR // SUB):
                q = pl.ds(i * TR + k * SUB, SUB)
                gated = yg[q, cols].astype(F32) + eg[q, cols].astype(F32) * far[q, cols]
                mean = jnp.sum(gated * gated, axis=1, keepdims=True) * (1.0 / GC)
                scale = lax.rsqrt(mean + EPSILON)
                ob[q, cols] = (gated * scale * gain).astype(BF16)
            outs.append(pltpu.make_async_copy(ob.at[r, cols], mo_ref.at[r, cols], out_s.at[2 * i + g]))
            outs[-1].start()
        if i == 0:
            came.wait()
            attention.start()
    for copy in outs:
        copy.wait()


def per_device(
    x_in, bc_in, gate_in, step_size, decay_rate, skip, conv_x, conv_bc, norm_gain, queries, keys_values, doc_lengths
):
    vm, hbm = pl.BlockSpec(memory_space=pltpu.VMEM), pl.BlockSpec(memory_space=pltpu.HBM)
    dma = pltpu.SemaphoreType.DMA
    V = pltpu.VMEM
    shape = jax.ShapeDtypeStruct
    main = pl.pallas_call(
        kernel,
        out_shape=(
            shape((T, INNER), BF16), shape((T, INNER), BF16), shape((T, 256), BF16),
            shape((2, ST, GC), BF16), shape((T, QH * AD), BF16),
        ),
        in_specs=[pl.BlockSpec(memory_space=pltpu.SMEM)] + [vm] * 4 + [hbm] * 6,
        out_specs=(hbm,) * 5,
        scratch_shapes=[
            V((HALO + T, INNER), BF16),
            V((HALO, INNER), BF16),
            V((T, 2, 256), BF16),
            V((HALO, 2, 256), BF16),
            V((HALO + T, 512), BF16),
            V((4, 512), F32),
            V((T, INNER), BF16),
            V((128, T), F32),
            V((T, 512), BF16),
            V((QH, T, 256), BF16),
            V((T, 2, 128), BF16),
            V((T, 2, 128), BF16),
            V((9, T, 384), BF16),
            V((HALO + T, 128), F32),
            V((HALO + T, 128), F32),
            V((T, 128), jnp.int32),
            V((3, T, 128), F32),
            V((T, INNER), BF16),
            V((NC, ST + CH, INNER), BF16),
            V((HALO, INNER), BF16),
            V((HALO, INNER), BF16),
            V((T, 256), BF16),
            V((2, NC, ST, CH), BF16),
            V((2, NC, CH, ST + CH), BF16),
            V((128, INNER), BF16),
            V((T, 128), F32),
            V((T, 128), F32),
            V((2, 4, ST + 16, NQ), BF16),
            V((4, ST + 16, NQ), BF16),
            V((4, ST + 16, NQ), BF16),
            V((2, 4, ST + 16, NQ), BF16),
            V((4, ST, NQ), BF16),
            V((4, ST, NQ), BF16),
            V((ST, GC), BF16),
            V((2, ST, GC), BF16),
            V((T, 128), BF16),
            V((T, 128), BF16),
            V((40, 128), F32),
            V((32, INNER), F32),
            V((T, 256), F32),
            V((T, 256), F32),
            V((T, INNER), BF16),
            V((T, INNER), BF16),
            V((T, 256), BF16),
            V((T, 512), BF16),
            V((T, 4 * T), F32),
            V((T, 4 * T), F32),
            V((T, 4 * T), BF16),
            V((T, 4 * T), BF16),
            V((QH, T, 128), F32),
            V((QH, T, 128), F32),
            V((T, 128), F32),
            V((T, 128), F32),
            V((QH, T, 128), F32),
            dma((6,)),
            dma((2, 3)),
            dma((2, 3)),
            dma((2,)),
            dma((2,)),
            dma((4,)),
            dma((4,)),
            dma((3, 2)),
            dma((3, 2)),
            dma((4,)),
            dma((4,)),
            dma((7,)),
            dma((7,)),
            dma((3,)),
            dma((3,)),
            dma((4,)),
            dma((4,)),
            dma,
            dma,
            dma((5,)),
        ],
        compiler_params=pltpu.CompilerParams(
            collective_id=0, has_side_effects=True, vmem_limit_bytes=60 * 1024 * 1024
        ),
        name="hybrid",
    )
    yg, eg, cc, tin, attended = main(
        doc_lengths, decay_rate, skip, conv_x, conv_bc, x_in, bc_in, gate_in, step_size.T, queries, keys_values)
    return pl.pallas_call(
        finish,
        out_shape=(shape((T, INNER), BF16), shape((T, QH * AD), BF16)),
        in_specs=[hbm] * 4 + [vm, hbm],
        out_specs=(hbm, hbm),
        scratch_shapes=[
            V((T, INNER), BF16), V((T, INNER), BF16), V((T, 256), BF16), V((2, ST, GC), BF16), V((T, QH * AD), BF16),
            V((T, INNER), F32), V((T, INNER), BF16), dma((3,)), dma((2, T // TR)), dma((2 * (T // TR) + 1,)),
        ],
        compiler_params=pltpu.CompilerParams(vmem_limit_bytes=60 * 1024 * 1024),
        name="finish",
    )(yg, eg, cc, tin, norm_gain, attended)


def solution(mesh):
    placed = (
        P("seq", "head"),
        P("seq", None, "head"),
        P("seq", "head"),
        P("seq", "head"),
        P("head"),
        P("head"),
        P(None, "head"),
        P(None, None, "head"),
        P("head"),
        P(("seq", "head"), None),
        P(("seq", "head"), None, None),
        P(),
    )
    return jax.shard_map(
        per_device,
        mesh=mesh,
        in_specs=placed,
        out_specs=(P("seq", "head"), P("seq", "head")),
        check_vma=False,
    )
```
